1024 devices in a mesh: dom: 128 (over z, x), sub: 8 (over y, core).
Axes of the slice: x: 4, y: 4, z: 32, core: 2. Of those that a mesh axis runs over, the one named last changes fastest.
Arguments:
- source_term: float32 [125, 524288], P(None, ('dom', 'sub')), may hold values from -20 to 20
- cell_levels: int32 [524288], P(('dom', 'sub')), may hold values from 0 to 2
- coefficient_ids: int32 [524288], P(('dom', 'sub')), may hold values from 0 to 63
- coefficient_values: float32 [64], replicated, may hold values from 0.3 to 3
- conforming_pairs: int32 [2, 983040], P(None, ('dom', 'sub')), may hold values from -1 to 3839, as said below
- hanging_coarse: int32 [524288], P(('dom', 'sub')), may hold values from -1 to 3071, as said below
- hanging_fine: int32 [4, 524288], P(None, ('dom', 'sub')), may hold values from -1 to 3071, as said below
Outputs:
- solution_field: float32 [125, 524288], P(None, ('dom', 'sub'))
- residual: float32 [125, 524288], P(None, ('dom', 'sub'))
The draws below stay inside these ranges and needn't reach their ends.
Inputs may be any that keep to these rules, and one draw needn't show every extreme that they name: `conforming_pairs`: every used pair lists its face and the opposite face (f + 3 mod 6) of a cell in the same block or within 64 cells of the block boundary in the neighbouring block; each pair appears also from the other side; entries with a -1 have -1 in both rows. `hanging_coarse`: A slot is used exactly when all four children of the matching slot in the block one step further along dom are used; the blocks with the last dom index have no used slots. `hanging_fine`: blocks with dom index 0 have no used slots; a used slot has four used children.
All inputs are finite; a program needn't handle non-finite values.
Results may differ from the reference program's by a relative error of at most 0.0033.
Values sent between devices are 32-bit elements; how exact they have to be, the bound alone decides.
No kernel may reach another device: no remote copies, remote signals or barrier semaphores. Data moves between devices by JAX's collectives and lax.ppermute only.
A program may use at most 32 MiB of HBM per device.

```python
import math
import jax
import jax.numpy as jnp
import numpy as np
from jax import lax

C_DEV = 512
NODES = 125
RIM = 64
QIN = 384
QX = 96
HSLOT = 512
NCOEF = 64
ITERS = 2
NPAIR = 960
BLOCKS = 1024
NCELL = 524288
N_SUB = 8


def hanging_counts(key):
    counts = jax.random.randint(jax.random.fold_in(key, 40), (BLOCKS,), 1, HSLOT + 1)
    counts = counts.at[0].set(HSLOT)
    block_index = jnp.arange(BLOCKS)
    return jnp.where(block_index < BLOCKS - N_SUB, counts, 0)


def draw_source_term(key, part):
    key = jax.random.fold_in(key, 5)
    first_key, second_key = jax.random.split(key, 2)
    position = jnp.arange(NCELL, dtype=jnp.float32) / max(NCELL - 1, 1)
    ramp = 1.0 + 2.0 * position
    roughness = jnp.exp(jax.random.uniform(second_key, (1, NCELL), minval=-0.69, maxval=0.69))
    noise = jax.random.truncated_normal(first_key, -3.0, 3.0, (NODES, NCELL))
    return (noise * roughness * ramp).astype(jnp.float32)


def draw_conforming_pairs(key, part):
    key = jax.random.fold_in(key, 31)
    subkeys = jax.random.split(key, 6)
    extent = C_DEV + 2 * RIM
    inner_first = jax.random.randint(subkeys[0], (BLOCKS, QIN), 0, C_DEV)
    inner_second = jax.random.randint(subkeys[1], (BLOCKS, QIN), 0, C_DEV)
    inner_face = jax.random.randint(subkeys[2], (BLOCKS, QIN), 0, 6)
    inner_opposite = (inner_face + 3) % 6
    first_local = inner_face * C_DEV + inner_first
    first_ext = inner_opposite * extent + inner_second + RIM
    second_local = inner_opposite * C_DEV + inner_second
    second_ext = inner_face * extent + inner_first + RIM
    cross_left = jax.random.randint(subkeys[3], (BLOCKS, QX), C_DEV - RIM, C_DEV)
    cross_right = jax.random.randint(subkeys[4], (BLOCKS, QX), 0, RIM)
    cross_face = jax.random.randint(subkeys[5], (BLOCKS, QX), 0, 6)
    cross_right = cross_right.at[0, 0].set(RIM - 1)
    cross_face = cross_face.at[0, 0].set(2)
    cross_opposite = (cross_face + 3) % 6
    block_index = jnp.arange(BLOCKS)[:, None]
    left_live = block_index < BLOCKS - 1
    left_first = jnp.where(left_live, cross_face * C_DEV + cross_left, -1)
    left_second = jnp.where(left_live, cross_opposite * extent + C_DEV + RIM + cross_right, -1)
    prior_left = jnp.roll(cross_left, 1, axis=0)
    prior_right = jnp.roll(cross_right, 1, axis=0)
    prior_face = jnp.roll(cross_face, 1, axis=0)
    prior_opposite = jnp.roll(cross_opposite, 1, axis=0)
    right_live = block_index > 0
    right_first = jnp.where(right_live, prior_opposite * C_DEV + prior_right, -1)
    right_second = jnp.where(right_live, prior_face * extent + prior_left - C_DEV + RIM, -1)
    firsts = jnp.concatenate([first_local, second_local, left_first, right_first], axis=1)
    seconds = jnp.concatenate([first_ext, second_ext, left_second, right_second], axis=1)
    return jnp.stack([firsts.reshape(-1), seconds.reshape(-1)]).astype(jnp.int32)


def draw_hanging_coarse(key, part):
    counts = hanging_counts(key)
    key = jax.random.fold_in(key, 21)
    face_codes = jax.random.randint(key, (BLOCKS, HSLOT), 0, 6 * C_DEV)
    slot_live = jnp.arange(HSLOT)[None, :] < counts[:, None]
    slot_codes = jnp.where(slot_live, face_codes, -1)
    slot_codes = slot_codes.at[0, 0].set(6 * C_DEV - 1)
    return slot_codes.reshape(-1).astype(jnp.int32)


def draw_hanging_fine(key, part):
    counts = hanging_counts(key)
    key = jax.random.fold_in(key, 22)
    shifted = jnp.concatenate([jnp.zeros((N_SUB,), counts.dtype), counts[:BLOCKS - N_SUB]])
    face_codes = jax.random.randint(key, (4, BLOCKS, HSLOT), 0, 6 * C_DEV)
    slot_live = jnp.arange(HSLOT)[None, None, :] < shifted[None, :, None]
    slot_codes = jnp.where(slot_live, face_codes, -1)
    slot_codes = slot_codes.at[0, N_SUB, 0].set(6 * C_DEV - 1)
    return slot_codes.reshape(4, -1).astype(jnp.int32)


def touch_ends(drawn, key, smallest, top_value):
    place = [jax.random.randint(jax.random.fold_in(key, axis), (), 0, length) for axis, length in enumerate(drawn.shape)]
    main_axis = drawn.shape.index(max(drawn.shape))
    next_to = place[:main_axis] + [(place[main_axis] + 1) % drawn.shape[main_axis]] + place[main_axis + 1:]
    return drawn.at[tuple(place)].set(smallest).at[tuple(next_to)].set(top_value)


def setup_inputs(seed: int = 0) -> dict:
    keys = jax.random.split(jax.random.key(seed), 8)
    return {
        "source_term": draw_source_term(jax.random.fold_in(keys[7], 71), 0),
        "cell_levels": touch_ends(jax.random.randint(keys[1], (NCELL,), 0, 3), jax.random.fold_in(keys[1], 1), 0, 2).astype(jnp.int32),
        "coefficient_ids": touch_ends(jax.random.randint(keys[2], (NCELL,), 0, NCOEF), jax.random.fold_in(keys[2], 1), 0, NCOEF - 1).astype(jnp.int32),
        "coefficient_values": jnp.clip(jnp.exp(jax.random.uniform(keys[3], (NCOEF,), jnp.float32, math.log(0.3), math.log(3.0))), 0.3, 3.0),
        "conforming_pairs": draw_conforming_pairs(jax.random.fold_in(keys[7], 71), 0),
        "hanging_coarse": draw_hanging_coarse(jax.random.fold_in(keys[7], 71), 0),
        "hanging_fine": draw_hanging_fine(jax.random.fold_in(keys[7], 71), 0),
    }


TAU_PENALTY = 2.0
SIGMA_MASS = 4.0
HIGHEST = lax.Precision.HIGHEST

def element_tables():
    points = np.array([-1.0, -np.sqrt(3.0 / 7.0), 0.0, np.sqrt(3.0 / 7.0), 1.0])
    weights = np.array([0.1, 49.0 / 90.0, 32.0 / 45.0, 49.0 / 90.0, 0.1])

    def lagrange(location):
        values = np.ones((location.shape[0], 5))
        for column in range(5):
            for other in range(5):
                if other != column:
                    values[:, column] *= (location - points[other]) / (points[column] - points[other])
        return values
    derivative = np.zeros((5, 5))
    for column in range(5):
        for other in range(5):
            if other != column:
                product = np.ones(5) / (points[column] - points[other])
                for remaining in range(5):
                    if remaining != column and remaining != other:
                        product = product * (points - points[remaining]) / (points[column] - points[remaining])
                derivative[:, column] += product
    stiffness = derivative.T @ (weights[:, None] * derivative)
    halves = [lagrange((points - 1.0) / 2.0), lagrange((points + 1.0) / 2.0)]
    interp = np.stack([np.kron(halves[first_half], halves[second_half]) for first_half in range(2) for second_half in range(2)])
    return (jnp.asarray(stiffness, jnp.float32), jnp.asarray(weights, jnp.float32), jnp.asarray(interp, jnp.float32))

def local_apply(nodal_cube, coefficient, cell_scale, stiffness, weights):
    weight_x = weights[:, None, None, None]
    weight_y = weights[None, :, None, None]
    weight_z = weights[None, None, :, None]
    along_x = jnp.einsum('ai,ijkc->ajkc', stiffness, nodal_cube, precision=HIGHEST) * weight_y * weight_z
    along_y = jnp.einsum('bj,ijkc->ibkc', stiffness, nodal_cube, precision=HIGHEST) * weight_x * weight_z
    along_z = jnp.einsum('dk,ijkc->ijdc', stiffness, nodal_cube, precision=HIGHEST) * weight_x * weight_y
    lumped = SIGMA_MASS * weight_x * weight_y * weight_z * (cell_scale * cell_scale * cell_scale)
    return coefficient * cell_scale * (along_x + along_y + along_z) + lumped * nodal_cube

def face_traces(nodal_cube):
    cell_count = nodal_cube.shape[3]
    slabs = [nodal_cube[0], nodal_cube[:, 0], nodal_cube[:, :, 0], nodal_cube[4], nodal_cube[:, 4], nodal_cube[:, :, 4]]
    return jnp.stack([face_slab.reshape(25, cell_count) for face_slab in slabs], axis=1)

def add_faces(nodal_cube, contribution):
    cell_count = nodal_cube.shape[3]
    pieces = contribution.reshape(5, 5, 6, cell_count)
    nodal_cube = nodal_cube.at[0].add(pieces[:, :, 0])
    nodal_cube = nodal_cube.at[:, 0].add(pieces[:, :, 1])
    nodal_cube = nodal_cube.at[:, :, 0].add(pieces[:, :, 2])
    nodal_cube = nodal_cube.at[4].add(pieces[:, :, 3])
    nodal_cube = nodal_cube.at[:, 4].add(pieces[:, :, 4])
    nodal_cube = nodal_cube.at[:, :, 4].add(pieces[:, :, 5])
    return nodal_cube.reshape(125, cell_count)

def operate(vector, coefficient, cell_scale, conforming_pairs, hanging_coarse, hanging_fine, tables):
    stiffness, weights, interp = tables
    nodal_cube = vector.reshape(5, 5, 5, NCELL)
    applied = local_apply(nodal_cube, coefficient, cell_scale, stiffness, weights)
    traces = face_traces(nodal_cube).reshape(25, 6 * NCELL)
    extent = C_DEV + 2 * RIM
    pair_block = jnp.arange(BLOCKS * NPAIR, dtype=jnp.int32) // NPAIR
    pair_live = conforming_pairs[0] >= 0
    first_safe = jnp.maximum(conforming_pairs[0], 0)
    second_safe = jnp.maximum(conforming_pairs[1], 0)
    first_index = first_safe // C_DEV * NCELL + pair_block * C_DEV + first_safe % C_DEV
    second_index = jnp.where(pair_live, second_safe // extent * NCELL + pair_block * C_DEV + second_safe % extent - RIM, 0)
    face_jump = TAU_PENALTY * (traces[:, first_index] - traces[:, second_index]) * pair_live.astype(jnp.float32)
    contribution = jnp.zeros_like(traces).at[:, first_index].add(face_jump)
    slot_block = jnp.arange(BLOCKS * HSLOT, dtype=jnp.int32) // HSLOT
    coarse_live = (hanging_coarse >= 0).astype(jnp.float32)
    coarse_safe = jnp.maximum(hanging_coarse, 0)
    coarse_index = coarse_safe // C_DEV * NCELL + slot_block * C_DEV + coarse_safe % C_DEV
    coarse_values = traces[:, coarse_index] * coarse_live
    arriving = jnp.concatenate([jnp.zeros((25, N_SUB * HSLOT), jnp.float32), coarse_values[:, :(BLOCKS - N_SUB) * HSLOT]], axis=1)
    fine_live = (hanging_fine >= 0).astype(jnp.float32)
    fine_safe = jnp.maximum(hanging_fine, 0)
    fine_index = fine_safe // C_DEV * NCELL + slot_block[None, :] * C_DEV + fine_safe % C_DEV
    fine_values = traces[:, fine_index] * fine_live
    predicted = jnp.einsum('sij,jh->ish', interp, arriving, precision=HIGHEST)
    fine_jump = TAU_PENALTY * (fine_values - predicted) * fine_live
    contribution = contribution.at[:, fine_index.reshape(-1)].add(fine_jump.reshape(25, -1))
    returned = -jnp.einsum('sji,jsh->ih', interp, fine_jump, precision=HIGHEST)
    going_back = jnp.concatenate([returned[:, N_SUB * HSLOT:], jnp.zeros((25, N_SUB * HSLOT), jnp.float32)], axis=1)
    contribution = contribution.at[:, coarse_index].add(going_back * coarse_live)
    return add_faces(applied, contribution.reshape(25, 6, NCELL))

def reference(source_term, cell_levels, coefficient_ids, coefficient_values, conforming_pairs, hanging_coarse, hanging_fine):
    tables = element_tables()
    coefficient = coefficient_values[coefficient_ids]
    cell_scale = jnp.exp2(-cell_levels.astype(jnp.float32))
    solution_field = jnp.zeros_like(source_term)
    residual = source_term
    direction = source_term
    norm_now = jnp.sum(residual * residual)
    for iteration in range(ITERS):
        image = operate(direction, coefficient, cell_scale, conforming_pairs, hanging_coarse, hanging_fine, tables)
        alpha = norm_now / jnp.sum(direction * image)
        solution_field = solution_field + alpha * direction
        residual = residual - alpha * image
        if iteration + 1 < ITERS:
            norm_next = jnp.sum(residual * residual)
            direction = residual + norm_next / norm_now * direction
            norm_now = norm_next
    return (solution_field, residual)
```

```python
import jax
import jax.numpy as jnp
import numpy as np
import ml_dtypes
from jax import lax
from jax.experimental import pallas as pl
from jax.experimental.pallas import tpu as pltpu
from jax.sharding import Mesh, PartitionSpec as P

CELLS = 512
RIM = 64
EXTENT = CELLS + 2 * RIM
PAIRS = 960
PAIR_SLOTS = 1024
SIDE = 128
FACE = 32
TRACE = 6 * FACE
FINE0 = PAIR_SLOTS
COARSE0 = PAIR_SLOTS + 4 * CELLS
SLOTS = COARSE0 + CELLS
CHUNK = 512
TAU_PENALTY = 2.0
SIGMA_MASS = 4.0
F32 = jnp.float32
BF16 = jnp.bfloat16
ALONG_ROWS = (((1,), (0,)), ((), ()))
ALONG_LANES = (((1,), (1,)), ((), ()))


def element_tables():
    points = np.array([-1.0, -np.sqrt(3.0 / 7.0), 0.0, np.sqrt(3.0 / 7.0), 1.0])
    weights = np.array([0.1, 49.0 / 90.0, 32.0 / 45.0, 49.0 / 90.0, 0.1])

    def lagrange(location):
        values = np.ones((location.shape[0], 5))
        for column in range(5):
            for other in range(5):
                if other != column:
                    values[:, column] *= (location - points[other]) / (
                        points[column] - points[other]
                    )
        return values

    derivative = np.zeros((5, 5))
    for column in range(5):
        for other in range(5):
            if other != column:
                product = np.ones(5) / (points[column] - points[other])
                for remaining in range(5):
                    if remaining != column and remaining != other:
                        product = (
                            product
                            * (points - points[remaining])
                            / (points[column] - points[remaining])
                        )
                derivative[:, column] += product
    stiffness = derivative.T @ (weights[:, None] * derivative)
    halves = [lagrange((points - 1.0) / 2.0), lagrange((points + 1.0) / 2.0)]
    interp = [np.kron(halves[a], halves[b]) for a in range(2) for b in range(2)]
    return stiffness, weights, interp


def two_parts(table):
    high = table.astype(np.float32).astype(ml_dtypes.bfloat16)
    low = (table - high.astype(np.float64)).astype(np.float32).astype(ml_dtypes.bfloat16)
    return high, low


def constant_tables():
    stiffness, weights, interp = element_tables()
    diag = np.diag(weights)

    def kron3(a, b, c):
        return np.kron(np.kron(a, b), c)

    local = np.zeros((128, 128))
    local[:125, :125] = (
        kron3(stiffness, diag, diag) + kron3(diag, stiffness, diag) + kron3(diag, diag, stiffness)
    )
    lumped = np.zeros((128, 1), np.float32)
    lumped[:125, 0] = SIGMA_MASS * np.einsum("i,j,k->ijk", weights, weights, weights).reshape(-1)
    node = np.arange(125).reshape(5, 5, 5)
    slabs = [node[0], node[:, 0], node[:, :, 0], node[4], node[:, 4], node[:, :, 4]]
    trace = np.zeros((TRACE, 128))
    for face, slab in enumerate(slabs):
        trace[face * FACE + np.arange(25), slab.reshape(-1)] = 1.0
    coarse = np.zeros((FACE, FACE))
    down = np.zeros((4 * FACE, FACE))
    for child, matrix in enumerate(interp):
        coarse[:25, :25] += matrix.T @ matrix
        down[child * FACE : child * FACE + 25, :25] = matrix
    return {
        "trace": trace.astype(ml_dtypes.bfloat16),
        "untrace": np.ascontiguousarray(trace.T).astype(ml_dtypes.bfloat16),
        "local": two_parts(local),
        "lumped": lumped,
        "coarse": two_parts(np.kron(np.eye(6), TAU_PENALTY * coarse)),
        "down": two_parts(-TAU_PENALTY * down),
        "up": two_parts(-TAU_PENALTY * np.ascontiguousarray(down.T)),
    }


def dot(a, b, dims=ALONG_ROWS):
    return lax.dot_general(a, b, dims, preferred_element_type=F32)


def split(value):
    high = value.astype(BF16)
    return high, (value - high.astype(F32)).astype(BF16)


def table_dot(high_ref, low_ref, value):
    high, low = split(value)
    table = high_ref[...]
    return dot(table, high) + dot(table, low) + dot(low_ref[...], high)


def face_traces(trace_ref, field):
    high, low = split(field)
    table = trace_ref[...]
    return dot(table, high), dot(table, low)


def one_hot(cell, rows):
    place = lax.broadcasted_iota(jnp.int32, (rows, cell.shape[1]), 0)
    return jnp.where(place == cell, 1.0, 0.0).astype(BF16)


def pick(gathered, face):
    total = None
    for f in range(6):
        both = gathered[f * FACE : (f + 1) * FACE] + gathered[TRACE + f * FACE : TRACE + (f + 1) * FACE]
        term = jnp.where(face == f, both, 0.0)
        total = term if total is None else total + term
    return total


def own_code(code):
    return code >> 9, code & (CELLS - 1)


def extended_code(code):
    face = jnp.where(code < 0, -1, 0)
    for f in range(1, 6):
        face = face + jnp.where(code >= f * EXTENT, 1, 0)
    return face, code - face * EXTENT - RIM


def padded_pairs(pairs_ref, codes):
    codes[...] = jnp.full_like(codes, -1)
    codes[0:2, 0:PAIRS] = pairs_ref[...]


def padded_field(field_ref, field):
    if field_ref.shape[0] == 128:
        return field_ref[...]
    field[...] = jnp.zeros_like(field)
    field[0:125, :] = field_ref[...]
    return field[...]


def gather_hanging(traces, hot, coarse_ref, fine_ref, up):
    rows = []
    for child in range(4):
        face, _ = own_code(fine_ref[child : child + 1, :])
        start = FINE0 + child * CELLS
        rows.append(pick(dot(traces, hot[:, start : start + CELLS]), face))
    face, _ = own_code(coarse_ref[...])
    send_coarse = pick(dot(traces, hot[:, COARSE0:SLOTS]), face)
    send_fine = table_dot(up[0], up[1], jnp.concatenate(rows, axis=0))
    return send_coarse, send_fine


def hot_hanging(hot, coarse_ref, fine_ref):
    for child in range(4):
        _, cell = own_code(fine_ref[child : child + 1, :])
        start = FINE0 + child * CELLS
        hot[:, start : start + CELLS] = one_hot(cell, CELLS)
    _, cell = own_code(coarse_ref[...])
    hot[:, COARSE0:SLOTS] = one_hot(cell, CELLS)


def stacked_traces(trace_ref, field):
    high, low = face_traces(trace_ref, field)
    return jnp.concatenate([high.astype(BF16), low.astype(BF16)], axis=0)


def first_kernel(
    field_ref, coarse_ref, fine_ref, trace_ref, uph_ref, upl_ref, send_coarse_ref, send_fine_ref, field, hot
):
    hot_hanging(hot, coarse_ref, fine_ref)
    traces = stacked_traces(trace_ref, padded_field(field_ref, field))
    send_coarse, send_fine = gather_hanging(traces, hot, coarse_ref, fine_ref, (uph_ref, upl_ref))
    send_coarse_ref[...] = send_coarse
    send_fine_ref[...] = send_fine


def middle_kernel(
    field_ref,
    pairs_ref,
    level_ref,
    id_ref,
    values_ref,
    trace_ref,
    lh_ref,
    ll_ref,
    lumped_ref,
    mh_ref,
    ml_ref,
    applied_ref,
    trace_out_ref,
    coarse_out_ref,
    partner_ref,
    field,
    codes,
):
    vector = padded_field(field_ref, field)
    padded_pairs(pairs_ref, codes)
    high, low = face_traces(trace_ref, vector)
    both = high + low
    trace_out_ref[...] = both
    coarse_out_ref[...] = table_dot(mh_ref, ml_ref, both)
    traces = jnp.concatenate([high.astype(BF16), low.astype(BF16)], axis=0)
    for start in range(0, PAIR_SLOTS, CHUNK):
        face, cell = extended_code(codes[1:2, start : start + CHUNK])
        partner_ref[:, start : start + CHUNK] = pick(dot(traces, one_hot(cell, CELLS)), face)
    place = lax.broadcasted_iota(jnp.int32, (values_ref.shape[1], CELLS), 0)
    lookup = jnp.where(place == id_ref[...], 1.0, 0.0)
    values = jnp.broadcast_to(values_ref[...], (8, values_ref.shape[1]))
    coefficient = lax.dot_general(
        values, lookup, ALONG_ROWS, precision=lax.Precision.HIGHEST, preferred_element_type=F32
    )[0:1]
    level = level_ref[...]
    scale = jnp.where(level == 0, 1.0, jnp.where(level == 1, 0.5, 0.25))
    stiff = table_dot(lh_ref, ll_ref, vector)
    cubed = scale * scale * scale
    applied_ref[...] = (coefficient * scale) * stiff + cubed * (lumped_ref[...] * vector)


def add_faces(
    pairs_ref,
    coarse_ref,
    fine_ref,
    applied_ref,
    trace_in_ref,
    coarse_in_ref,
    partner_ref,
    below_ref,
    above_ref,
    arriving_ref,
    returned_ref,
    trace_ref,
    untrace_ref,
    dh_ref,
    dl_ref,
    codes,
    sides,
    hot,
    spread,
):
    padded_pairs(pairs_ref, codes)
    hot_hanging(hot, coarse_ref, fine_ref)
    if below_ref.shape[0] != 128:
        sides[...] = jnp.zeros_like(sides)
    rows = below_ref.shape[0]
    sides[0:rows, 0:SIDE] = below_ref[...]
    sides[0:rows, SIDE : 2 * SIDE] = above_ref[...]
    side_traces = stacked_traces(trace_ref, sides[...])

    def put(start, value, face, coarse):
        width = value.shape[1]
        high = value.astype(BF16).astype(F32)
        low = value - high
        for f in range(6):
            live = face == f
            spread[f * FACE : (f + 1) * FACE, start : start + width] = jnp.where(live, high, 0.0).astype(BF16)
            spread[TRACE + f * FACE : TRACE + (f + 1) * FACE, start : start + width] = jnp.where(
                live, low, 0.0
            ).astype(BF16)
        row = lax.broadcasted_iota(jnp.int32, (16, width), 0)
        spread[2 * TRACE : 2 * TRACE + 16, start : start + width] = jnp.where(
            row == (face + 8 if coarse else face), 1.0, 0.0
        ).astype(BF16)

    for start in range(0, PAIR_SLOTS, CHUNK):
        face, cell = extended_code(codes[1:2, start : start + CHUNK])
        place = jnp.where(cell < 0, cell + SIDE, jnp.where(cell >= CELLS, cell + (SIDE - CELLS), -1))
        place = jnp.where(face < 0, -1, place)
        partner = partner_ref[:, start : start + CHUNK] + pick(
            dot(side_traces, one_hot(place, 2 * SIDE)), face
        )
        face, cell = own_code(codes[0:1, start : start + CHUNK])
        hot[:, start : start + CHUNK] = one_hot(cell, CELLS)
        put(start, -TAU_PENALTY * partner, face, False)
    predicted = table_dot(dh_ref, dl_ref, arriving_ref[...])
    for child in range(4):
        face, _ = own_code(fine_ref[child : child + 1, :])
        put(FINE0 + child * CELLS, predicted[child * FACE : (child + 1) * FACE], face, False)
    face, _ = own_code(coarse_ref[...])
    put(COARSE0, returned_ref[...], face, True)
    added = dot(spread[...], hot[...], ALONG_LANES)
    pieces = []
    for f in range(6):
        rows = slice(f * FACE, (f + 1) * FACE)
        fine_count = added[2 * TRACE + f : 2 * TRACE + f + 1]
        coarse_count = added[2 * TRACE + 8 + f : 2 * TRACE + 9 + f]
        pieces.append(
            added[f * FACE : (f + 1) * FACE]
            + added[TRACE + f * FACE : TRACE + (f + 1) * FACE]
            + (TAU_PENALTY * fine_count) * trace_in_ref[rows, :]
            + coarse_count * coarse_in_ref[rows, :]
        )
    high, low = split(jnp.concatenate(pieces, axis=0))
    untrace = untrace_ref[...]
    return applied_ref[...] + (dot(untrace, high) + dot(untrace, low))


def image_kernel(*refs):
    (coarse_ref, fine_ref, trace_ref) = (refs[1], refs[2], refs[11])
    uph_ref, upl_ref = refs[15:17]
    out_ref, low_ref, high_ref, send_coarse_ref, send_fine_ref = refs[17:22]
    codes, sides, hot, spread = refs[22:]
    image = add_faces(*refs[:15], codes, sides, hot, spread)
    out_ref[...] = image
    low_ref[...] = image[:, 0:SIDE]
    high_ref[...] = image[:, CELLS - SIDE :]
    traces = stacked_traces(trace_ref, image)
    send_coarse, send_fine = gather_hanging(traces, hot, coarse_ref, fine_ref, (uph_ref, upl_ref))
    send_coarse_ref[...] = send_coarse
    send_fine_ref[...] = send_fine


def total(value):
    return jnp.sum(jnp.sum(value, axis=0, keepdims=True), axis=1, keepdims=True)


def moments_kernel(*refs):
    source_ref, image_ref = refs[15:17]
    out_ref, sums_ref = refs[17:19]
    codes, sides, hot, spread = refs[19:]
    second = add_faces(*refs[:15], codes, sides, hot, spread)
    out_ref[...] = second
    source = source_ref[...]
    image = image_ref[...]
    products = [
        source * source,
        source * image[0:125],
        image * image,
        source * second[0:125],
        image * second,
    ]
    lane = lax.broadcasted_iota(jnp.int32, (1, 128), 1)
    line = jnp.zeros((1, 128), F32)
    for index, product in enumerate(products):
        line = line + jnp.where(lane == index, total(product), 0.0)
    sums_ref[...] = jnp.broadcast_to(line[None], sums_ref.shape)


def last_kernel(sums_ref, source_ref, image_ref, second_ref, solution_ref, residual_ref):
    line = jnp.sum(sums_ref[...], axis=0)
    rr, rw, ww, ru, wu = (line[:, i : i + 1] for i in range(5))
    first_step = rr / rw
    rr_next = rr - 2.0 * first_step * rw + first_step * first_step * ww
    grown = 1.0 + rr_next / rr
    curvature = (
        grown * grown * rw - first_step * grown * (ru + ww) + first_step * first_step * wu
    )
    second_step = rr_next / curvature
    p = first_step + second_step * grown
    q = second_step * first_step
    source = source_ref[...]
    image = image_ref[0:125, :]
    solution_ref[...] = p * source - q * image
    residual_ref[...] = source - p * image + q * second_ref[0:125, :]


def call(kernel, out_shapes, scratch, *operands, name):
    space = pl.BlockSpec(memory_space=pltpu.VMEM)
    return pl.pallas_call(
        kernel,
        out_shape=[jax.ShapeDtypeStruct(shape, F32) for shape in out_shapes],
        in_specs=[space] * len(operands),
        out_specs=[space] * len(out_shapes),
        scratch_shapes=scratch,
        compiler_params=pltpu.CompilerParams(vmem_limit_bytes=48 * 1024 * 1024),
        name=name,
    )(*operands)


FIELD = pltpu.VMEM((128, CELLS), F32)
CODES = pltpu.VMEM((8, PAIR_SLOTS), jnp.int32)
SIDES = pltpu.VMEM((128, 2 * SIDE), F32)
HOT = pltpu.VMEM((CELLS, SLOTS), BF16)
SPREAD = pltpu.VMEM((2 * TRACE + 16, SLOTS), BF16)


def shifted(value, axes, step):
    count = lax.axis_size(axes)
    return lax.ppermute(
        value, axes, [(i, i + step) for i in range(count) if 0 <= i + step < count]
    )


def on_device(source, levels, ids, values, pairs, coarse, fine):
    tables = constant_tables()
    block = ("z", "x", "y", "core")
    dom = ("z", "x")
    plane = ("x", "y", "core")
    levels, ids, values, coarse = (a.reshape(1, -1) for a in (levels, ids, values, coarse))
    trace, untrace = tables["trace"], tables["untrace"]

    def middle(field):
        return call(
            middle_kernel,
            [(128, CELLS), (TRACE, CELLS), (TRACE, CELLS), (FACE, PAIR_SLOTS)],
            [FIELD, CODES],
            field,
            pairs,
            levels,
            ids,
            values,
            trace,
            *tables["local"],
            tables["lumped"],
            *tables["coarse"],
            name="middle",
        )

    below = shifted(source[:, CELLS - SIDE :], block, 1)
    above = shifted(source[:, :SIDE], block, -1)
    send_coarse, send_fine = call(
        first_kernel,
        [(FACE, CELLS)] * 2,
        [FIELD, HOT],
        source,
        coarse,
        fine,
        trace,
        *tables["up"],
        name="first",
    )
    arriving = shifted(send_coarse, dom, 1)
    returned = shifted(send_fine, dom, -1)
    scratch = [CODES, SIDES, HOT, SPREAD]
    image, low, high, send_coarse, send_fine = call(
        image_kernel,
        [(128, CELLS), (128, SIDE), (128, SIDE), (FACE, CELLS), (FACE, CELLS)],
        scratch,
        pairs,
        coarse,
        fine,
        *middle(source),
        below,
        above,
        arriving,
        returned,
        trace,
        untrace,
        *tables["down"],
        *tables["up"],
        name="image",
    )
    below = shifted(high, block, 1)
    above = shifted(low, block, -1)
    arriving = shifted(send_coarse, dom, 1)
    returned = shifted(send_fine, dom, -1)
    in_plane = lax.axis_size(plane)
    along_z = lax.axis_size("z")
    second, sums = call(
        moments_kernel,
        [(128, CELLS), (in_plane, 1, 128)],
        scratch,
        pairs,
        coarse,
        fine,
        *middle(image),
        below,
        above,
        arriving,
        returned,
        trace,
        untrace,
        *tables["down"],
        source,
        image,
        name="moments",
    )
    sums = lax.all_to_all(sums, plane, 0, 0, tiled=True)
    sums = jnp.broadcast_to(jnp.sum(sums, axis=0, keepdims=True), (along_z, 1, 128))
    sums = lax.all_to_all(sums, "z", 0, 0, tiled=True)
    return tuple(call(last_kernel, [source.shape] * 2, [], sums, source, image, second, name="last"))


def solution(mesh):
    dom, sub = mesh.devices.shape
    axes = ("z", "x", "y", "core")
    fine_mesh = Mesh(mesh.devices.reshape(dom // 4, 4, sub // 2, 2), axes)
    return jax.shard_map(
        on_device,
        mesh=fine_mesh,
        in_specs=(
            P(None, axes),
            P(axes),
            P(axes),
            P(),
            P(None, axes),
            P(axes),
            P(None, axes),
        ),
        out_specs=(P(None, axes), P(None, axes)),
        check_vma=False,
    )
```

```python
import jax
import jax.numpy as jnp
import numpy as np
import ml_dtypes
from jax import lax
from jax.experimental import pallas as pl
from jax.experimental.pallas import tpu as pltpu
from jax.sharding import Mesh, PartitionSpec as P

CELLS = 512
RIM = 64
EXTENT = CELLS + 2 * RIM
PAIRS = 960
PAIR_SLOTS = 1024
SIDE = 128
FACE = 32
TRACE = 6 * FACE
FINE0 = PAIR_SLOTS
COARSE0 = PAIR_SLOTS + 4 * CELLS
SLOTS = COARSE0 + CELLS
CHUNK = 512
FINE_ROW = 2
COARSE_ROW = 6
TAU_PENALTY = 2.0
SIGMA_MASS = 4.0
BLOCK = ("z", "x", "y", "core")
DOM = ("z", "x")
PLANE = ("x", "y", "core")
F32 = jnp.float32
BF16 = jnp.bfloat16
ALONG_ROWS = (((1,), (0,)), ((), ()))
ALONG_LANES = (((1,), (1,)), ((), ()))


def element_tables():
    points = np.array([-1.0, -np.sqrt(3.0 / 7.0), 0.0, np.sqrt(3.0 / 7.0), 1.0])
    weights = np.array([0.1, 49.0 / 90.0, 32.0 / 45.0, 49.0 / 90.0, 0.1])

    def lagrange(location):
        values = np.ones((location.shape[0], 5))
        for column in range(5):
            for other in range(5):
                if other != column:
                    values[:, column] *= (location - points[other]) / (
                        points[column] - points[other]
                    )
        return values

    derivative = np.zeros((5, 5))
    for column in range(5):
        for other in range(5):
            if other != column:
                product = np.ones(5) / (points[column] - points[other])
                for remaining in range(5):
                    if remaining != column and remaining != other:
                        product = (
                            product
                            * (points - points[remaining])
                            / (points[column] - points[remaining])
                        )
                derivative[:, column] += product
    stiffness = derivative.T @ (weights[:, None] * derivative)
    halves = [lagrange((points - 1.0) / 2.0), lagrange((points + 1.0) / 2.0)]
    interp = [np.kron(halves[a], halves[b]) for a in range(2) for b in range(2)]
    return stiffness, weights, interp


def two_parts(table):
    high = table.astype(np.float32).astype(ml_dtypes.bfloat16)
    low = (table - high.astype(np.float64)).astype(np.float32).astype(ml_dtypes.bfloat16)
    return high, low


PLACES = {
    "trace": [(0, 0)],
    "up": [(192, 0), (192, 128)],
    "untrace": [(224, 0)],
    "coarse": [(352, 0), (544, 0)],
    "local": [(736, 0), (736, 128)],
    "down": [(864, 0), (864, 128)],
    "lumped": [(992, 0), (992, 128)],
}
FIRST_ROWS = 224
TABLE_ROWS = 1120


def packed_table():
    stiffness, weights, interp = element_tables()
    diag = np.diag(weights)

    def kron3(a, b, c):
        return np.kron(np.kron(a, b), c)

    local = np.zeros((128, 128))
    local[:125, :125] = (
        kron3(stiffness, diag, diag) + kron3(diag, stiffness, diag) + kron3(diag, diag, stiffness)
    )
    lumped = np.zeros((128, 1))
    lumped[:125, 0] = SIGMA_MASS * np.einsum("i,j,k->ijk", weights, weights, weights).reshape(-1)
    node = np.arange(125).reshape(5, 5, 5)
    slabs = [node[0], node[:, 0], node[:, :, 0], node[4], node[:, 4], node[:, :, 4]]
    trace = np.zeros((TRACE, 128))
    for face, slab in enumerate(slabs):
        trace[face * FACE + np.arange(25), slab.reshape(-1)] = 1.0
    coarse = np.zeros((FACE, FACE))
    down = np.zeros((4 * FACE, FACE))
    for child, matrix in enumerate(interp):
        coarse[:25, :25] += matrix.T @ matrix
        down[child * FACE : child * FACE + 25, :25] = matrix
    table = np.zeros((TABLE_ROWS, 256))
    places = {
        "trace": trace,
        "untrace": trace.T,
        "local": local,
        "coarse": np.kron(np.eye(6), TAU_PENALTY * coarse),
        "down": -TAU_PENALTY * down,
        "up": -TAU_PENALTY * down.T,
        "lumped": lumped,
    }
    for name, value in places.items():
        parts = [value] if name.endswith("trace") else two_parts(value)
        for (row, lane), part in zip(PLACES[name], parts):
            table[row : row + value.shape[0], lane : lane + value.shape[1]] = part
    return table.astype(ml_dtypes.bfloat16)


def views(table):
    def view(name, rows, lanes):
        return [table.at[row : row + rows, lane : lane + lanes] for row, lane in PLACES[name]]

    return {
        "trace": view("trace", TRACE, 128)[0],
        "untrace": view("untrace", 128, TRACE)[0],
        "local": view("local", 128, 128),
        "coarse": view("coarse", TRACE, TRACE),
        "down": view("down", 4 * FACE, FACE),
        "up": view("up", FACE, 128),
        "lumped": view("lumped", 128, 1),
    }


def dot(a, b, dims=ALONG_ROWS):
    return lax.dot_general(a, b, dims, preferred_element_type=F32)


def split(value):
    high = value.astype(BF16)
    return high, (value - high.astype(F32)).astype(BF16)


def table_dot(parts, value):
    high, low = split(value)
    table = parts[0][...]
    return dot(table, high) + dot(table, low) + dot(parts[1][...], high)


def face_traces(trace_ref, field):
    high, low = split(field)
    table = trace_ref[...]
    return dot(table, high), dot(table, low)


def one_hot(cell, rows):
    place = lax.broadcasted_iota(jnp.int32, (rows, cell.shape[1]), 0)
    return jnp.where(place == cell, 1.0, 0.0).astype(BF16)


def pick(gathered, face):
    total = None
    for f in range(6):
        both = gathered[f * FACE : (f + 1) * FACE] + gathered[TRACE + f * FACE : TRACE + (f + 1) * FACE]
        term = jnp.where(face == f, both, 0.0)
        total = term if total is None else total + term
    return total


def own_code(code):
    return code >> 9, code & (CELLS - 1)


def extended_code(code):
    face = jnp.where(code < 0, -1, 0)
    for f in range(1, 6):
        face = face + jnp.where(code >= f * EXTENT, 1, 0)
    return face, code - face * EXTENT - RIM


def padded_field(field_ref, field):
    if field_ref.shape[0] == 128:
        return field_ref[...]
    field[...] = jnp.zeros_like(field)
    field[0:125, :] = field_ref[...]
    return field[...]


def fine_code(codes, child):
    return own_code(codes[FINE_ROW + child : FINE_ROW + child + 1, 0:CELLS])


def coarse_code(codes):
    return own_code(codes[COARSE_ROW : COARSE_ROW + 1, 0:CELLS])


def gather_hanging(traces, hot, codes, up):
    rows = []
    for child in range(4):
        face, _ = fine_code(codes, child)
        start = FINE0 + child * CELLS
        rows.append(pick(dot(traces, hot[:, start : start + CELLS]), face))
    face, _ = coarse_code(codes)
    send_coarse = pick(dot(traces, hot[:, COARSE0:SLOTS]), face)
    send_fine = table_dot(up, jnp.concatenate(rows, axis=0))
    return send_coarse, send_fine


def hot_hanging(hot, codes):
    for child in range(4):
        _, cell = fine_code(codes, child)
        start = FINE0 + child * CELLS
        hot[:, start : start + CELLS] = one_hot(cell, CELLS)
    _, cell = coarse_code(codes)
    hot[:, COARSE0:SLOTS] = one_hot(cell, CELLS)


def stacked_traces(trace_ref, field):
    high, low = face_traces(trace_ref, field)
    return jnp.concatenate([high.astype(BF16), low.astype(BF16)], axis=0)


def swaps(low, high, send_coarse, send_fine, rim_chip_ref, dom_odd_ref, rim_core_ref, dom_even_ref):
    first_core = lax.axis_index("core") == 0
    even_dom = lax.axis_index("x") % 2 == 0
    rim_core_ref[...] = jnp.where(first_core, high, low)
    rim_chip_ref[...] = jnp.where(first_core, low, high)
    dom_even_ref[...] = jnp.where(even_dom, send_coarse, send_fine)
    dom_odd_ref[...] = jnp.where(even_dom, send_fine, send_coarse)


def first_kernel(*refs):
    field_in, level_in, id_in, values_in, pairs_in, coarse_in, fine_in, table_in = refs[:8]
    outs, codes, scales = refs[8:12], refs[12], refs[13]
    source, levels, ids, values, pairs, coarse, fine, table, field, hot, sems = refs[14:]
    moves = [
        (coarse_in, coarse),
        (fine_in, fine),
        (field_in, source),
        (table_in.at[0:FIRST_ROWS], table),
        (level_in, levels),
        (id_in, ids),
        (values_in, values),
        (pairs_in, pairs),
    ]
    copies = [pltpu.make_async_copy(*move, sems.at[i]) for i, move in enumerate(moves)]
    for copy in copies:
        copy.start()
    codes[...] = jnp.full_like(codes, -1)
    copies[0].wait()
    codes[COARSE_ROW : COARSE_ROW + 1, 0:CELLS] = coarse[...]
    copies[1].wait()
    codes[FINE_ROW : FINE_ROW + 4, 0:CELLS] = fine[...]
    hot_hanging(hot, codes)
    copies[2].wait()
    copies[3].wait()
    vector = padded_field(source, field)
    traces = stacked_traces(table.at[0:TRACE, 0:128], vector)
    up = [table.at[row : row + FACE, lane : lane + 128] for row, lane in PLACES["up"]]
    send_coarse, send_fine = gather_hanging(traces, hot, codes, up)
    swaps(vector[:, 0:SIDE], vector[:, CELLS - SIDE :], send_coarse, send_fine, *outs)
    for copy in copies[4:]:
        copy.wait()
    codes[0:2, 0:PAIRS] = pairs[...]
    place = lax.broadcasted_iota(jnp.int32, (values.shape[1], CELLS), 0)
    lookup = jnp.where(place == ids[...], 1.0, 0.0)
    coefficient = lax.dot_general(
        jnp.broadcast_to(values[...], (8, values.shape[1])),
        lookup,
        ALONG_ROWS,
        precision=lax.Precision.HIGHEST,
        preferred_element_type=F32,
    )
    level = levels[...]
    scale = jnp.where(level == 0, 1.0, jnp.where(level == 1, 0.5, 0.25))
    row = lax.broadcasted_iota(jnp.int32, scales.shape, 0)
    scales[...] = jnp.where(row == 0, coefficient * scale, scale * scale * scale)


def middle_kernel(
    field_ref, codes, scales, table_ref, applied_ref, trace_out_ref, coarse_out_ref, partner_ref, field
):
    table = views(table_ref)
    vector = padded_field(field_ref, field)
    high, low = face_traces(table["trace"], vector)
    both = high + low
    trace_out_ref[...] = both
    coarse_out_ref[...] = table_dot(table["coarse"], both)
    traces = jnp.concatenate([high.astype(BF16), low.astype(BF16)], axis=0)
    for start in range(0, PAIR_SLOTS, CHUNK):
        face, cell = extended_code(codes[1:2, start : start + CHUNK])
        partner_ref[:, start : start + CHUNK] = pick(dot(traces, one_hot(cell, CELLS)), face)
    stiff = table_dot(table["local"], vector)
    lumped = table["lumped"][0][...].astype(F32) + table["lumped"][1][...].astype(F32)
    applied_ref[...] = scales[0:1, :] * stiff + scales[1:2, :] * (lumped * vector)


def add_faces(
    codes,
    table_ref,
    applied_ref,
    trace_in_ref,
    coarse_in_ref,
    partner_ref,
    rim_chip_ref,
    dom_odd_ref,
    rim_core_ref,
    dom_even_ref,
    sides,
    hot,
    spread,
):
    table = views(table_ref)
    hot_hanging(hot, codes)
    first_core = lax.axis_index("core") == 0
    even_dom = lax.axis_index("x") % 2 == 0
    sides[:, 0:SIDE] = jnp.where(first_core, rim_chip_ref[...], rim_core_ref[...])
    sides[:, SIDE : 2 * SIDE] = jnp.where(first_core, rim_core_ref[...], rim_chip_ref[...])
    arriving = jnp.where(even_dom, dom_odd_ref[...], dom_even_ref[...])
    returned = jnp.where(even_dom, dom_even_ref[...], dom_odd_ref[...])
    side_traces = stacked_traces(table["trace"], sides[...])

    def put(start, value, face, coarse):
        width = value.shape[1]
        high = value.astype(BF16).astype(F32)
        low = value - high
        for f in range(6):
            live = face == f
            spread[f * FACE : (f + 1) * FACE, start : start + width] = jnp.where(live, high, 0.0).astype(BF16)
            spread[TRACE + f * FACE : TRACE + (f + 1) * FACE, start : start + width] = jnp.where(
                live, low, 0.0
            ).astype(BF16)
        row = lax.broadcasted_iota(jnp.int32, (16, width), 0)
        spread[2 * TRACE : 2 * TRACE + 16, start : start + width] = jnp.where(
            row == (face + 8 if coarse else face), 1.0, 0.0
        ).astype(BF16)

    for start in range(0, PAIR_SLOTS, CHUNK):
        face, cell = extended_code(codes[1:2, start : start + CHUNK])
        place = jnp.where(cell < 0, cell + SIDE, jnp.where(cell >= CELLS, cell + (SIDE - CELLS), -1))
        place = jnp.where(face < 0, -1, place)
        partner = partner_ref[:, start : start + CHUNK] + pick(
            dot(side_traces, one_hot(place, 2 * SIDE)), face
        )
        face, cell = own_code(codes[0:1, start : start + CHUNK])
        hot[:, start : start + CHUNK] = one_hot(cell, CELLS)
        put(start, -TAU_PENALTY * partner, face, False)
    predicted = table_dot(table["down"], arriving)
    for child in range(4):
        face, _ = fine_code(codes, child)
        put(FINE0 + child * CELLS, predicted[child * FACE : (child + 1) * FACE], face, False)
    face, _ = coarse_code(codes)
    put(COARSE0, returned, face, True)
    added = dot(spread[...], hot[...], ALONG_LANES)
    pieces = []
    for f in range(6):
        rows = slice(f * FACE, (f + 1) * FACE)
        fine_count = added[2 * TRACE + f : 2 * TRACE + f + 1]
        coarse_count = added[2 * TRACE + 8 + f : 2 * TRACE + 9 + f]
        pieces.append(
            added[f * FACE : (f + 1) * FACE]
            + added[TRACE + f * FACE : TRACE + (f + 1) * FACE]
            + (TAU_PENALTY * fine_count) * trace_in_ref[rows, :]
            + coarse_count * coarse_in_ref[rows, :]
        )
    high, low = split(jnp.concatenate(pieces, axis=0))
    untrace = table["untrace"][...]
    return applied_ref[...] + (dot(untrace, high) + dot(untrace, low))


def image_kernel(*refs):
    codes, table = refs[0], views(refs[1])
    image = add_faces(*refs[:10], *refs[15:])
    refs[10][...] = image
    traces = stacked_traces(table["trace"], image)
    send_coarse, send_fine = gather_hanging(traces, refs[16], codes, table["up"])
    swaps(image[:, 0:SIDE], image[:, CELLS - SIDE :], send_coarse, send_fine, *refs[11:15])


def total(value):
    return jnp.sum(jnp.sum(value, axis=0, keepdims=True), axis=1, keepdims=True)


def moments_kernel(*refs):
    source_ref, image_ref, out_ref, sums_ref = refs[10:14]
    second = add_faces(*refs[:10], *refs[14:])
    out_ref[...] = second
    source = source_ref[...]
    image = image_ref[...]
    products = [
        source * source,
        source * image[0:125],
        image * image,
        source * second[0:125],
        image * second,
    ]
    lane = lax.broadcasted_iota(jnp.int32, (1, 128), 1)
    line = jnp.zeros((1, 128), F32)
    for index, product in enumerate(products):
        line = line + jnp.where(lane == index, total(product), 0.0)
    sums_ref[...] = jnp.broadcast_to(line[None], sums_ref.shape)


def last_kernel(sums_ref, source_ref, image_ref, second_ref, solution_ref, residual_ref):
    line = jnp.sum(sums_ref[...], axis=0)
    rr, rw, ww, ru, wu = (line[:, i : i + 1] for i in range(5))
    first_step = rr / rw
    rr_next = rr - 2.0 * first_step * rw + first_step * first_step * ww
    grown = 1.0 + rr_next / rr
    curvature = (
        grown * grown * rw - first_step * grown * (ru + ww) + first_step * first_step * wu
    )
    second_step = rr_next / curvature
    p = first_step + second_step * grown
    q = second_step * first_step
    source = source_ref[...]
    image = image_ref[0:125, :]
    solution_ref[...] = p * source - q * image
    residual_ref[...] = source - p * image + q * second_ref[0:125, :]


def call(kernel, out_shapes, scratch, *operands, name, space=pltpu.VMEM, limit=48):
    return pl.pallas_call(
        kernel,
        out_shape=[jax.ShapeDtypeStruct(shape, F32) for shape in out_shapes]
        if isinstance(out_shapes[0], tuple)
        else out_shapes,
        in_specs=[pl.BlockSpec(memory_space=space)] * len(operands),
        out_specs=[pl.BlockSpec(memory_space=pltpu.VMEM)] * len(out_shapes),
        scratch_shapes=scratch,
        compiler_params=pltpu.CompilerParams(vmem_limit_bytes=limit * 1024 * 1024),
        name=name,
    )(*operands)


FIELD = pltpu.VMEM((128, CELLS), F32)
SIDES = pltpu.VMEM((128, 2 * SIDE), F32)
HOT = pltpu.VMEM((CELLS, SLOTS), BF16)
SPREAD = pltpu.VMEM((2 * TRACE + 16, SLOTS), BF16)


def swapped(value, axes, first):
    count = lax.axis_size(axes)
    pairs = [(i, i + 1) for i in range(first, count - 1, 2)]
    return lax.ppermute(value, axes, pairs + [(above, below) for below, above in pairs])


def exchange(rim_chip, dom_odd, rim_core, dom_even):
    rim_chip = swapped(rim_chip, BLOCK, 1)
    dom_odd = swapped(dom_odd, DOM, 1)
    dom_even = swapped(dom_even, DOM, 0)
    rim_core = swapped(rim_core, BLOCK, 0)
    return rim_chip, dom_odd, rim_core, dom_even


def summed_over_blocks(sums):
    in_plane, along_z = lax.axis_size(PLANE), lax.axis_size("z")
    sums = lax.all_to_all(sums, PLANE, 0, 0, tiled=True)
    diagonal = [
        (z * in_plane + place, (z + place) % along_z * in_plane + place)
        for z in range(along_z)
        for place in range(along_z)
    ]
    other = lax.ppermute(jnp.sum(sums, axis=0, keepdims=True), BLOCK, diagonal)
    return lax.all_to_all(jnp.broadcast_to(other, sums.shape), PLANE, 0, 0, tiled=True)


def on_device(source, levels, ids, values, pairs, coarse, fine):
    levels, ids, values, coarse = (a.reshape(1, -1) for a in (levels, ids, values, coarse))
    table = jnp.asarray(packed_table())
    sends = [jax.ShapeDtypeStruct(shape, F32) for shape in [(128, SIDE), (FACE, CELLS)] * 2]
    params = (source, levels, ids, values, pairs, coarse, fine)
    *swapping, codes, scales = call(
        first_kernel,
        [
            *sends,
            jax.ShapeDtypeStruct((8, PAIR_SLOTS), jnp.int32),
            jax.ShapeDtypeStruct((8, CELLS), F32),
        ],
        [
            *(pltpu.VMEM(a.shape, a.dtype) for a in params),
            pltpu.VMEM((FIRST_ROWS, 256), BF16),
            FIELD,
            HOT,
            pltpu.SemaphoreType.DMA((8,)),
        ],
        *params,
        table,
        name="first",
        space=pl.ANY,
        limit=63,
    )

    def middle(field):
        shapes = [(128, CELLS), (TRACE, CELLS), (TRACE, CELLS), (FACE, PAIR_SLOTS)]
        return call(middle_kernel, shapes, [FIELD], field, codes, scales, table, name="middle")

    scratch = [SIDES, HOT, SPREAD]
    arrived = exchange(*swapping)
    image, *swapping = call(
        image_kernel,
        [jax.ShapeDtypeStruct((128, CELLS), F32), *sends],
        scratch,
        codes,
        table,
        *middle(source),
        *arrived,
        name="image",
    )
    arrived = exchange(*swapping)
    second, sums = call(
        moments_kernel,
        [(128, CELLS), (lax.axis_size(PLANE), 1, 128)],
        scratch,
        codes,
        table,
        *middle(image),
        *arrived,
        source,
        image,
        name="moments",
    )
    sums = summed_over_blocks(sums)
    return tuple(call(last_kernel, [source.shape] * 2, [], sums, source, image, second, name="last"))


def solution(mesh):
    dom, sub = mesh.devices.shape
    axes = BLOCK
    fine_mesh = Mesh(mesh.devices.reshape(dom // 4, 4, sub // 2, 2), axes)
    return jax.shard_map(
        on_device,
        mesh=fine_mesh,
        in_specs=(
            P(None, axes),
            P(axes),
            P(axes),
            P(),
            P(None, axes),
            P(axes),
            P(None, axes),
        ),
        out_specs=(P(None, axes), P(None, axes)),
        check_vma=False,
    )
```

```python
import jax
import jax.numpy as jnp
import numpy as np
import ml_dtypes
from jax import lax
from jax.experimental import pallas as pl
from jax.experimental.pallas import tpu as pltpu
from jax.sharding import Mesh, PartitionSpec as P

CELLS = 512
RIM = 64
EXTENT = CELLS + 2 * RIM
PAIRS = 960
PAIR_SLOTS = 1024
SIDE = 128
FACE = 32
TRACE = 6 * FACE
FINE0 = PAIR_SLOTS
COARSE0 = PAIR_SLOTS + 4 * CELLS
SLOTS = COARSE0 + CELLS
CHUNK = 512
FINE_ROW = 2
COARSE_ROW = 6
SCALE_ROW = 8
PACKED = (16, PAIR_SLOTS)
TAU_PENALTY = 2.0
SIGMA_MASS = 4.0
BLOCK = ("z", "x", "y", "core")
DOM = ("z", "x")
PLANE = ("x", "y", "core")
F32 = jnp.float32
BF16 = jnp.bfloat16
ALONG_ROWS = (((1,), (0,)), ((), ()))
ALONG_LANES = (((1,), (1,)), ((), ()))


def element_tables():
    points = np.array([-1.0, -np.sqrt(3.0 / 7.0), 0.0, np.sqrt(3.0 / 7.0), 1.0])
    weights = np.array([0.1, 49.0 / 90.0, 32.0 / 45.0, 49.0 / 90.0, 0.1])

    def lagrange(location):
        values = np.ones((location.shape[0], 5))
        for column in range(5):
            for other in range(5):
                if other != column:
                    values[:, column] *= (location - points[other]) / (
                        points[column] - points[other]
                    )
        return values

    derivative = np.zeros((5, 5))
    for column in range(5):
        for other in range(5):
            if other != column:
                product = np.ones(5) / (points[column] - points[other])
                for remaining in range(5):
                    if remaining != column and remaining != other:
                        product = (
                            product
                            * (points - points[remaining])
                            / (points[column] - points[remaining])
                        )
                derivative[:, column] += product
    stiffness = derivative.T @ (weights[:, None] * derivative)
    halves = [lagrange((points - 1.0) / 2.0), lagrange((points + 1.0) / 2.0)]
    interp = [np.kron(halves[a], halves[b]) for a in range(2) for b in range(2)]
    return stiffness, weights, interp


def two_parts(table):
    high = table.astype(np.float32).astype(ml_dtypes.bfloat16)
    low = (table - high.astype(np.float64)).astype(np.float32).astype(ml_dtypes.bfloat16)
    return high, low


PLACES = {
    "trace": [(0, 0)],
    "up": [(192, 0), (192, 128)],
    "untrace": [(224, 0)],
    "coarse": [(352, 0), (544, 0)],
    "local": [(736, 0), (736, 128)],
    "down": [(864, 0), (864, 128)],
    "lumped": [(992, 0), (992, 128)],
}
FIRST_ROWS = 224
TABLE_ROWS = 1120


def packed_table():
    stiffness, weights, interp = element_tables()
    diag = np.diag(weights)

    def kron3(a, b, c):
        return np.kron(np.kron(a, b), c)

    local = np.zeros((128, 128))
    local[:125, :125] = (
        kron3(stiffness, diag, diag) + kron3(diag, stiffness, diag) + kron3(diag, diag, stiffness)
    )
    lumped = np.zeros((128, 1))
    lumped[:125, 0] = SIGMA_MASS * np.einsum("i,j,k->ijk", weights, weights, weights).reshape(-1)
    node = np.arange(125).reshape(5, 5, 5)
    slabs = [node[0], node[:, 0], node[:, :, 0], node[4], node[:, 4], node[:, :, 4]]
    trace = np.zeros((TRACE, 128))
    for face, slab in enumerate(slabs):
        trace[face * FACE + np.arange(25), slab.reshape(-1)] = 1.0
    coarse = np.zeros((FACE, FACE))
    down = np.zeros((4 * FACE, FACE))
    for child, matrix in enumerate(interp):
        coarse[:25, :25] += matrix.T @ matrix
        down[child * FACE : child * FACE + 25, :25] = matrix
    table = np.zeros((TABLE_ROWS, 256))
    places = {
        "trace": trace,
        "untrace": trace.T,
        "local": local,
        "coarse": np.kron(np.eye(6), TAU_PENALTY * coarse),
        "down": -TAU_PENALTY * down,
        "up": -TAU_PENALTY * down.T,
        "lumped": lumped,
    }
    for name, value in places.items():
        parts = [value] if name.endswith("trace") else two_parts(value)
        for (row, lane), part in zip(PLACES[name], parts):
            table[row : row + value.shape[0], lane : lane + value.shape[1]] = part
    return table.astype(ml_dtypes.bfloat16)


def views(table):
    def view(name, rows, lanes):
        return [table.at[row : row + rows, lane : lane + lanes] for row, lane in PLACES[name]]

    return {
        "trace": view("trace", TRACE, 128)[0],
        "untrace": view("untrace", 128, TRACE)[0],
        "local": view("local", 128, 128),
        "coarse": view("coarse", TRACE, TRACE),
        "down": view("down", 4 * FACE, FACE),
        "up": view("up", FACE, 128),
        "lumped": view("lumped", 128, 1),
    }


def dot(a, b, dims=ALONG_ROWS):
    return lax.dot_general(a, b, dims, preferred_element_type=F32)


def split(value):
    high = value.astype(BF16)
    return high, (value - high.astype(F32)).astype(BF16)


def table_dot(parts, value):
    high, low = split(value)
    table = parts[0][...]
    return dot(table, high) + dot(table, low) + dot(parts[1][...], high)


def face_traces(trace_ref, field):
    high, low = split(field)
    table = trace_ref[...]
    return dot(table, high), dot(table, low)


def one_hot(cell, rows):
    place = lax.broadcasted_iota(jnp.int32, (rows, cell.shape[1]), 0)
    return jnp.where(place == cell, 1.0, 0.0).astype(BF16)


def pick(gathered, face):
    total = None
    for f in range(6):
        both = gathered[f * FACE : (f + 1) * FACE] + gathered[TRACE + f * FACE : TRACE + (f + 1) * FACE]
        term = jnp.where(face == f, both, 0.0)
        total = term if total is None else total + term
    return total


def own_code(code):
    code = code.astype(jnp.int32)
    return code >> 9, code & (CELLS - 1)


def extended_code(code):
    code = code.astype(jnp.int32)
    face = jnp.where(code < 0, -1, 0)
    for f in range(1, 6):
        face = face + jnp.where(code >= f * EXTENT, 1, 0)
    return face, code - face * EXTENT - RIM


def padded_field(field_ref, field):
    if field_ref.shape[0] == 128:
        return field_ref[...]
    field[...] = jnp.zeros_like(field)
    field[0:125, :] = field_ref[...]
    return field[...]


def fine_code(codes, child):
    return own_code(codes[FINE_ROW + child : FINE_ROW + child + 1, 0:CELLS])


def coarse_code(codes):
    return own_code(codes[COARSE_ROW : COARSE_ROW + 1, 0:CELLS])


def gather_hanging(traces, hot, codes, up):
    rows = []
    for child in range(4):
        face, _ = fine_code(codes, child)
        start = FINE0 + child * CELLS
        rows.append(pick(dot(traces, hot[:, start : start + CELLS]), face))
    face, _ = coarse_code(codes)
    send_coarse = pick(dot(traces, hot[:, COARSE0:SLOTS]), face)
    send_fine = table_dot(up, jnp.concatenate(rows, axis=0))
    return send_coarse, send_fine


def hot_pairs(hot, codes):
    for start in range(0, PAIR_SLOTS, CHUNK):
        _, cell = own_code(codes[0:1, start : start + CHUNK])
        hot[:, start : start + CHUNK] = one_hot(cell, CELLS)


def hot_hanging(hot, codes):
    for child in range(4):
        _, cell = fine_code(codes, child)
        start = FINE0 + child * CELLS
        hot[:, start : start + CELLS] = one_hot(cell, CELLS)
    _, cell = coarse_code(codes)
    hot[:, COARSE0:SLOTS] = one_hot(cell, CELLS)


def stacked_traces(trace_ref, field):
    high, low = face_traces(trace_ref, field)
    return jnp.concatenate([high.astype(BF16), low.astype(BF16)], axis=0)


def swaps(low, high, send_coarse, send_fine, rim_chip_ref, dom_odd_ref, dom_even_ref, rim_core_ref):
    first_core = lax.axis_index("core") == 0
    even_dom = lax.axis_index("x") % 2 == 0
    rim_core_ref[...] = jnp.where(first_core, high, low)
    rim_chip_ref[...] = jnp.where(first_core, low, high)
    dom_even_ref[...] = jnp.where(even_dom, send_coarse, send_fine)
    dom_odd_ref[...] = jnp.where(even_dom, send_fine, send_coarse)


def first_kernel(*refs):
    field_in, level_in, id_in, values_in, pairs_in, coarse_in, fine_in, table_in = refs[:8]
    outs, codes = refs[8:12], refs[12]
    source, levels, ids, values, pairs, coarse, fine, table, field, hot, sems = refs[13:]
    moves = [
        (coarse_in, coarse),
        (fine_in, fine),
        (field_in, source),
        (table_in.at[0:FIRST_ROWS], table),
        (level_in, levels),
        (id_in, ids),
        (values_in, values),
        (pairs_in, pairs),
    ]
    copies = [pltpu.make_async_copy(*move, sems.at[i]) for i, move in enumerate(moves)]
    for copy in copies:
        copy.start()
    codes[...] = jnp.full(codes.shape, -1.0, F32)
    copies[0].wait()
    codes[COARSE_ROW : COARSE_ROW + 1, 0:CELLS] = coarse[...].astype(F32)
    copies[1].wait()
    codes[FINE_ROW : FINE_ROW + 4, 0:CELLS] = fine[...].astype(F32)
    hot_hanging(hot, codes)
    copies[2].wait()
    copies[3].wait()
    vector = padded_field(source, field)
    traces = stacked_traces(table.at[0:TRACE, 0:128], vector)
    up = [table.at[row : row + FACE, lane : lane + 128] for row, lane in PLACES["up"]]
    send_coarse, send_fine = gather_hanging(traces, hot, codes, up)
    swaps(vector[:, 0:SIDE], vector[:, CELLS - SIDE :], send_coarse, send_fine, *outs)
    for copy in copies[4:]:
        copy.wait()
    codes[0:2, 0:PAIRS] = pairs[...].astype(F32)
    place = lax.broadcasted_iota(jnp.int32, (values.shape[1], CELLS), 0)
    lookup = jnp.where(place == ids[...], 1.0, 0.0)
    coefficient = lax.dot_general(
        jnp.broadcast_to(values[...], (8, values.shape[1])),
        lookup,
        ALONG_ROWS,
        precision=lax.Precision.HIGHEST,
        preferred_element_type=F32,
    )
    level = levels[...]
    scale = jnp.where(level == 0, 1.0, jnp.where(level == 1, 0.5, 0.25))
    codes[SCALE_ROW : SCALE_ROW + 1, 0:CELLS] = coefficient[0:1] * scale
    codes[SCALE_ROW + 1 : SCALE_ROW + 2, 0:CELLS] = scale * scale * scale


def middle_kernel(
    field_ref, codes, table_ref, applied_ref, trace_out_ref, coarse_out_ref, partner_ref, field
):
    table = views(table_ref)
    vector = padded_field(field_ref, field)
    high, low = face_traces(table["trace"], vector)
    both = high + low
    trace_out_ref[...] = both
    coarse_out_ref[...] = table_dot(table["coarse"], both)
    traces = jnp.concatenate([high.astype(BF16), low.astype(BF16)], axis=0)
    for start in range(0, PAIR_SLOTS, CHUNK):
        face, cell = extended_code(codes[1:2, start : start + CHUNK])
        partner_ref[:, start : start + CHUNK] = pick(dot(traces, one_hot(cell, CELLS)), face)
    stiff = table_dot(table["local"], vector)
    lumped = table["lumped"][0][...].astype(F32) + table["lumped"][1][...].astype(F32)
    factor = codes[SCALE_ROW : SCALE_ROW + 1, 0:CELLS]
    cubed = codes[SCALE_ROW + 1 : SCALE_ROW + 2, 0:CELLS]
    applied_ref[...] = factor * stiff + cubed * (lumped * vector)


def add_faces(
    codes,
    table_ref,
    applied_ref,
    trace_in_ref,
    coarse_in_ref,
    partner_ref,
    rim_chip_ref,
    dom_odd_ref,
    dom_even_ref,
    rim_core_ref,
    sides,
    hot,
    spread,
):
    table = views(table_ref)
    hot_pairs(hot, codes)
    hot_hanging(hot, codes)
    first_core = lax.axis_index("core") == 0
    even_dom = lax.axis_index("x") % 2 == 0
    sides[:, 0:SIDE] = jnp.where(first_core, rim_chip_ref[...], rim_core_ref[...])
    sides[:, SIDE : 2 * SIDE] = jnp.where(first_core, rim_core_ref[...], rim_chip_ref[...])
    arriving = jnp.where(even_dom, dom_odd_ref[...], dom_even_ref[...])
    returned = jnp.where(even_dom, dom_even_ref[...], dom_odd_ref[...])
    side_traces = stacked_traces(table["trace"], sides[...])

    def put(start, value, face, coarse):
        width = value.shape[1]
        high = value.astype(BF16).astype(F32)
        low = value - high
        for f in range(6):
            live = face == f
            spread[f * FACE : (f + 1) * FACE, start : start + width] = jnp.where(live, high, 0.0).astype(BF16)
            spread[TRACE + f * FACE : TRACE + (f + 1) * FACE, start : start + width] = jnp.where(
                live, low, 0.0
            ).astype(BF16)
        row = lax.broadcasted_iota(jnp.int32, (16, width), 0)
        spread[2 * TRACE : 2 * TRACE + 16, start : start + width] = jnp.where(
            row == (face + 8 if coarse else face), 1.0, 0.0
        ).astype(BF16)

    for start in range(0, PAIR_SLOTS, CHUNK):
        face, cell = extended_code(codes[1:2, start : start + CHUNK])
        place = jnp.where(cell < 0, cell + SIDE, jnp.where(cell >= CELLS, cell + (SIDE - CELLS), -1))
        place = jnp.where(face < 0, -1, place)
        partner = partner_ref[:, start : start + CHUNK] + pick(
            dot(side_traces, one_hot(place, 2 * SIDE)), face
        )
        face, _ = own_code(codes[0:1, start : start + CHUNK])
        put(start, -TAU_PENALTY * partner, face, False)
    predicted = table_dot(table["down"], arriving)
    for child in range(4):
        face, _ = fine_code(codes, child)
        put(FINE0 + child * CELLS, predicted[child * FACE : (child + 1) * FACE], face, False)
    face, _ = coarse_code(codes)
    put(COARSE0, returned, face, True)
    added = dot(spread[...], hot[...], ALONG_LANES)
    pieces = []
    for f in range(6):
        rows = slice(f * FACE, (f + 1) * FACE)
        fine_count = added[2 * TRACE + f : 2 * TRACE + f + 1]
        coarse_count = added[2 * TRACE + 8 + f : 2 * TRACE + 9 + f]
        pieces.append(
            added[f * FACE : (f + 1) * FACE]
            + added[TRACE + f * FACE : TRACE + (f + 1) * FACE]
            + (TAU_PENALTY * fine_count) * trace_in_ref[rows, :]
            + coarse_count * coarse_in_ref[rows, :]
        )
    high, low = split(jnp.concatenate(pieces, axis=0))
    untrace = table["untrace"][...]
    return applied_ref[...] + (dot(untrace, high) + dot(untrace, low))


def image_kernel(*refs):
    codes, table = refs[0], views(refs[1])
    image = add_faces(*refs[:10], *refs[15:])
    refs[10][...] = image
    traces = stacked_traces(table["trace"], image)
    send_coarse, send_fine = gather_hanging(traces, refs[16], codes, table["up"])
    swaps(image[:, 0:SIDE], image[:, CELLS - SIDE :], send_coarse, send_fine, *refs[11:15])


def total(value):
    return jnp.sum(jnp.sum(value, axis=0, keepdims=True), axis=1, keepdims=True)


def moments_kernel(*refs):
    source_ref, image_ref, out_ref, sums_ref = refs[10:14]
    second = add_faces(*refs[:10], *refs[14:])
    out_ref[...] = second
    source = source_ref[...]
    image = image_ref[...]
    products = [
        source * source,
        source * image[0:125],
        image * image,
        source * second[0:125],
        image * second,
    ]
    lane = lax.broadcasted_iota(jnp.int32, (1, 128), 1)
    line = jnp.zeros((1, 128), F32)
    for index, product in enumerate(products):
        line = line + jnp.where(lane == index, total(product), 0.0)
    sums_ref[...] = jnp.broadcast_to(line[None], sums_ref.shape)


def last_kernel(sums_ref, source_ref, image_ref, second_ref, solution_ref, residual_ref):
    line = jnp.sum(sums_ref[...], axis=0)
    rr, rw, ww, ru, wu = (line[:, i : i + 1] for i in range(5))
    first_step = rr / rw
    rr_next = rr - 2.0 * first_step * rw + first_step * first_step * ww
    grown = 1.0 + rr_next / rr
    curvature = (
        grown * grown * rw - first_step * grown * (ru + ww) + first_step * first_step * wu
    )
    second_step = rr_next / curvature
    p = first_step + second_step * grown
    q = second_step * first_step
    source = source_ref[...]
    image = image_ref[0:125, :]
    solution_ref[...] = p * source - q * image
    residual_ref[...] = source - p * image + q * second_ref[0:125, :]


def call(kernel, out_shapes, scratch, *operands, name, space=pltpu.VMEM, limit=48):
    return pl.pallas_call(
        kernel,
        out_shape=[jax.ShapeDtypeStruct(shape, F32) for shape in out_shapes],
        in_specs=[pl.BlockSpec(memory_space=space)] * len(operands),
        out_specs=[pl.BlockSpec(memory_space=pltpu.VMEM)] * len(out_shapes),
        scratch_shapes=scratch,
        compiler_params=pltpu.CompilerParams(vmem_limit_bytes=limit * 1024 * 1024),
        name=name,
    )(*operands)


FIELD = pltpu.VMEM((128, CELLS), F32)
SIDES = pltpu.VMEM((128, 2 * SIDE), F32)
HOT = pltpu.VMEM((CELLS, SLOTS), BF16)
SPREAD = pltpu.VMEM((2 * TRACE + 16, SLOTS), BF16)


def swapped(value, axes, first):
    count = lax.axis_size(axes)
    pairs = [(i, i + 1) for i in range(first, count - 1, 2)]
    return lax.ppermute(value, axes, pairs + [(above, below) for below, above in pairs])


def exchange(rim_chip, dom_odd, dom_even, rim_core):
    rim_chip = swapped(rim_chip, BLOCK, 1)
    dom_odd = swapped(dom_odd, DOM, 1)
    dom_even = swapped(dom_even, DOM, 0)
    rim_core = swapped(rim_core, BLOCK, 0)
    return rim_chip, dom_odd, dom_even, rim_core


def summed_over_blocks(sums):
    in_plane, along_z = lax.axis_size(PLANE), lax.axis_size("z")
    sums = lax.all_to_all(sums, PLANE, 0, 0, tiled=True)
    diagonal = [
        (z * in_plane + place, (z + place) % along_z * in_plane + place)
        for z in range(along_z)
        for place in range(along_z)
    ]
    other = lax.ppermute(jnp.sum(sums, axis=0, keepdims=True), BLOCK, diagonal)
    return lax.all_to_all(jnp.broadcast_to(other, sums.shape), PLANE, 0, 0, tiled=True)


def on_device(source, levels, ids, values, pairs, coarse, fine):
    levels, ids, values, coarse = (a.reshape(1, -1) for a in (levels, ids, values, coarse))
    table = jnp.asarray(packed_table())
    sends = [(128, SIDE), (FACE, CELLS), (FACE, CELLS), (128, SIDE)]
    params = (source, levels, ids, values, pairs, coarse, fine)
    *swapping, codes = call(
        first_kernel,
        [*sends, PACKED],
        [
            *(pltpu.VMEM(a.shape, a.dtype) for a in params),
            pltpu.VMEM((FIRST_ROWS, 256), BF16),
            FIELD,
            HOT,
            pltpu.SemaphoreType.DMA((8,)),
        ],
        *params,
        table,
        name="first",
        space=pl.ANY,
        limit=63,
    )

    arrays = [(128, CELLS), (TRACE, CELLS), (TRACE, CELLS), (FACE, PAIR_SLOTS)]
    scratch = [SIDES, HOT, SPREAD]
    arrived = exchange(*swapping)
    own = call(middle_kernel, arrays, [FIELD], source, codes, table, name="middle")
    image, *swapping = call(
        image_kernel,
        [(128, CELLS), *sends],
        scratch,
        codes,
        table,
        *own,
        *arrived,
        name="image",
    )
    arrived = exchange(*swapping)
    own = call(middle_kernel, arrays, [FIELD], image, codes, table, name="middle")
    second, sums = call(
        moments_kernel,
        [(128, CELLS), (lax.axis_size(PLANE), 1, 128)],
        scratch,
        codes,
        table,
        *own,
        *arrived,
        source,
        image,
        name="moments",
    )
    sums = summed_over_blocks(sums)
    return tuple(call(last_kernel, [source.shape] * 2, [], sums, source, image, second, name="last"))


def solution(mesh):
    dom, sub = mesh.devices.shape
    axes = BLOCK
    fine_mesh = Mesh(mesh.devices.reshape(dom // 4, 4, sub // 2, 2), axes)
    return jax.shard_map(
        on_device,
        mesh=fine_mesh,
        in_specs=(
            P(None, axes),
            P(axes),
            P(axes),
            P(),
            P(None, axes),
            P(axes),
            P(None, axes),
        ),
        out_specs=(P(None, axes), P(None, axes)),
        check_vma=False,
    )
```

```python
import jax
import jax.numpy as jnp
import numpy as np
import ml_dtypes
from jax import lax
from jax.experimental import pallas as pl
from jax.experimental.pallas import tpu as pltpu
from jax.sharding import Mesh, PartitionSpec as P

CELLS = 512
RIM = 64
EXTENT = CELLS + 2 * RIM
PAIRS = 960
PAIR_SLOTS = 1024
SIDE = 128
FACE = 32
MAIN = 24
TAIL = 6 * MAIN
STACK = TAIL + 8
TRACE = 160
FINE0 = PAIR_SLOTS
COARSE0 = PAIR_SLOTS + 4 * CELLS
SLOTS = COARSE0 + CELLS
CHUNK = 512
FINE_ROW = 2
COARSE_ROW = 6
SCALE_ROW = 8
PACKED = (16, PAIR_SLOTS)
TAU_PENALTY = 2.0
SIGMA_MASS = 4.0
BLOCK = ("z", "x", "y", "core")
DOM = ("z", "x")
PLANE = ("x", "y", "core")
F32 = jnp.float32
BF16 = jnp.bfloat16
ALONG_ROWS = (((1,), (0,)), ((), ()))
ALONG_LANES = (((1,), (1,)), ((), ()))


def element_tables():
    points = np.array([-1.0, -np.sqrt(3.0 / 7.0), 0.0, np.sqrt(3.0 / 7.0), 1.0])
    weights = np.array([0.1, 49.0 / 90.0, 32.0 / 45.0, 49.0 / 90.0, 0.1])

    def lagrange(location):
        values = np.ones((location.shape[0], 5))
        for column in range(5):
            for other in range(5):
                if other != column:
                    values[:, column] *= (location - points[other]) / (
                        points[column] - points[other]
                    )
        return values

    derivative = np.zeros((5, 5))
    for column in range(5):
        for other in range(5):
            if other != column:
                product = np.ones(5) / (points[column] - points[other])
                for remaining in range(5):
                    if remaining != column and remaining != other:
                        product = (
                            product
                            * (points - points[remaining])
                            / (points[column] - points[remaining])
                        )
                derivative[:, column] += product
    stiffness = derivative.T @ (weights[:, None] * derivative)
    halves = [lagrange((points - 1.0) / 2.0), lagrange((points + 1.0) / 2.0)]
    interp = [np.kron(halves[a], halves[b]) for a in range(2) for b in range(2)]
    return stiffness, weights, interp


def two_parts(table):
    high = table.astype(np.float32).astype(ml_dtypes.bfloat16)
    low = (table - high.astype(np.float64)).astype(np.float32).astype(ml_dtypes.bfloat16)
    return high, low


PLACES = {
    "trace": [(0, 0)],
    "up": [(160, 0), (160, 128)],
    "untrace": [(192, 0)],
    "coarse": [(320, 0), (480, 0)],
    "local": [(640, 0), (640, 128)],
    "down": [(768, 0), (768, 128)],
    "lumped": [(896, 0), (896, 128)],
}
FIRST_ROWS = 192
TABLE_ROWS = 1024


def packed_table():
    stiffness, weights, interp = element_tables()
    diag = np.diag(weights)

    def kron3(a, b, c):
        return np.kron(np.kron(a, b), c)

    local = np.zeros((128, 128))
    local[:125, :125] = (
        kron3(stiffness, diag, diag) + kron3(diag, stiffness, diag) + kron3(diag, diag, stiffness)
    )
    lumped = np.zeros((128, 1))
    lumped[:125, 0] = SIGMA_MASS * np.einsum("i,j,k->ijk", weights, weights, weights).reshape(-1)
    node = np.arange(125).reshape(5, 5, 5)
    slabs = [node[0], node[:, 0], node[:, :, 0], node[4], node[:, 4], node[:, :, 4]]
    stacked = np.concatenate([np.arange(6)[:, None] * MAIN + np.arange(MAIN), TAIL + np.arange(6)[:, None]], axis=1)
    trace = np.zeros((TRACE, 128))
    for face, slab in enumerate(slabs):
        trace[stacked[face], slab.reshape(-1)] = 1.0
    coarse = np.zeros((25, 25))
    down = np.zeros((4 * FACE, FACE))
    for child, matrix in enumerate(interp):
        coarse += matrix.T @ matrix
        down[child * FACE : child * FACE + 25, :25] = matrix
    coarse_stack = np.zeros((TRACE, TRACE))
    for rows in stacked:
        coarse_stack[np.ix_(rows, rows)] = TAU_PENALTY * coarse
    table = np.zeros((TABLE_ROWS, 256))
    places = {
        "trace": trace,
        "untrace": trace.T,
        "local": local,
        "coarse": coarse_stack,
        "down": -TAU_PENALTY * down,
        "up": -TAU_PENALTY * down.T,
        "lumped": lumped,
    }
    for name, value in places.items():
        parts = [value] if name.endswith("trace") else two_parts(value)
        for (row, lane), part in zip(PLACES[name], parts):
            table[row : row + value.shape[0], lane : lane + value.shape[1]] = part
    return table.astype(ml_dtypes.bfloat16)


def views(table):
    def view(name, rows, lanes):
        return [table.at[row : row + rows, lane : lane + lanes] for row, lane in PLACES[name]]

    return {
        "trace": view("trace", TRACE, 128)[0],
        "untrace": view("untrace", 128, TRACE)[0],
        "local": view("local", 128, 128),
        "coarse": view("coarse", TRACE, TRACE),
        "down": view("down", 4 * FACE, FACE),
        "up": view("up", FACE, 128),
        "lumped": view("lumped", 128, 1),
    }


def dot(a, b, dims=ALONG_ROWS):
    return lax.dot_general(a, b, dims, preferred_element_type=F32)


def split(value):
    high = value.astype(BF16)
    return high, (value - high.astype(F32)).astype(BF16)


def table_dot(parts, value):
    high, low = split(value)
    table = parts[0][...]
    return dot(table, high) + dot(table, low) + dot(parts[1][...], high)


def face_traces(trace_ref, field):
    high, low = split(field)
    table = trace_ref[...]
    return dot(table, high), dot(table, low)


def one_hot(cell, rows):
    place = lax.broadcasted_iota(jnp.int32, (rows, cell.shape[1]), 0)
    return jnp.where(place == cell, 1.0, 0.0).astype(BF16)


def pick(gathered, face):
    both = gathered[0:STACK] + gathered[STACK : 2 * STACK]
    main = None
    for f in range(6):
        term = jnp.where(face == f, both[f * MAIN : (f + 1) * MAIN], 0.0)
        main = term if main is None else main + term
    row = lax.broadcasted_iota(jnp.int32, (8, both.shape[1]), 0)
    last = jnp.sum(jnp.where(row == face, both[TAIL:STACK], 0.0), axis=0, keepdims=True)
    return jnp.concatenate([main, jnp.where(row == 0, last, 0.0)], axis=0)


def stack(value, face):
    row = lax.broadcasted_iota(jnp.int32, (8, value.shape[1]), 0)
    pieces = [jnp.where(face == f, value[0:MAIN], 0.0) for f in range(6)]
    return pieces + [jnp.where(row == face, value[MAIN : MAIN + 1], 0.0)]


def own_code(code):
    code = code.astype(jnp.int32)
    return code >> 9, code & (CELLS - 1)


def extended_code(code):
    code = code.astype(jnp.int32)
    face = jnp.where(code < 0, -1, 0)
    for f in range(1, 6):
        face = face + jnp.where(code >= f * EXTENT, 1, 0)
    return face, code - face * EXTENT - RIM


def padded_field(field_ref, field):
    if field_ref.shape[0] == 128:
        return field_ref[...]
    field[...] = jnp.zeros_like(field)
    field[0:125, :] = field_ref[...]
    return field[...]


def fine_code(codes, child):
    return own_code(codes[FINE_ROW + child : FINE_ROW + child + 1, 0:CELLS])


def coarse_code(codes):
    return own_code(codes[COARSE_ROW : COARSE_ROW + 1, 0:CELLS])


def gather_hanging(traces, hot, codes, up):
    rows = []
    for child in range(4):
        face, _ = fine_code(codes, child)
        start = FINE0 + child * CELLS
        rows.append(pick(dot(traces, hot[:, start : start + CELLS]), face))
    face, _ = coarse_code(codes)
    send_coarse = pick(dot(traces, hot[:, COARSE0:SLOTS]), face)
    send_fine = table_dot(up, jnp.concatenate(rows, axis=0))
    return send_coarse, send_fine


def hot_pairs(hot, codes):
    for start in range(0, PAIR_SLOTS, CHUNK):
        _, cell = own_code(codes[0:1, start : start + CHUNK])
        hot[:, start : start + CHUNK] = one_hot(cell, CELLS)


def hot_hanging(hot, codes):
    for child in range(4):
        _, cell = fine_code(codes, child)
        start = FINE0 + child * CELLS
        hot[:, start : start + CELLS] = one_hot(cell, CELLS)
    _, cell = coarse_code(codes)
    hot[:, COARSE0:SLOTS] = one_hot(cell, CELLS)


def joined(high, low):
    return jnp.concatenate([high[0:STACK], low[0:STACK]], axis=0).astype(BF16)


def stacked_traces(trace_ref, field):
    return joined(*face_traces(trace_ref, field))


def swaps(low, high, send_coarse, send_fine, rim_chip_ref, dom_odd_ref, dom_even_ref, rim_core_ref):
    first_core = lax.axis_index("core") == 0
    even_dom = lax.axis_index("x") % 2 == 0
    rim_core_ref[...] = jnp.where(first_core, high, low)
    rim_chip_ref[...] = jnp.where(first_core, low, high)
    dom_even_ref[...] = jnp.where(even_dom, send_coarse, send_fine)
    dom_odd_ref[...] = jnp.where(even_dom, send_fine, send_coarse)


def first_kernel(*refs):
    field_in, level_in, id_in, values_in, pairs_in, coarse_in, fine_in, table_in = refs[:8]
    outs, codes = refs[8:12], refs[12]
    source, levels, ids, values, pairs, coarse, fine, table, field, hot, sems = refs[13:]
    moves = [
        (coarse_in, coarse),
        (fine_in, fine),
        (field_in, source),
        (table_in.at[0:FIRST_ROWS], table),
        (level_in, levels),
        (id_in, ids),
        (values_in, values),
        (pairs_in, pairs),
    ]
    copies = [pltpu.make_async_copy(*move, sems.at[i]) for i, move in enumerate(moves)]
    for copy in copies:
        copy.start()
    codes[...] = jnp.full(codes.shape, -1.0, F32)
    copies[0].wait()
    codes[COARSE_ROW : COARSE_ROW + 1, 0:CELLS] = coarse[...].astype(F32)
    copies[1].wait()
    codes[FINE_ROW : FINE_ROW + 4, 0:CELLS] = fine[...].astype(F32)
    hot_hanging(hot, codes)
    copies[2].wait()
    copies[3].wait()
    vector = padded_field(source, field)
    traces = stacked_traces(table.at[0:TRACE, 0:128], vector)
    up = [table.at[row : row + FACE, lane : lane + 128] for row, lane in PLACES["up"]]
    send_coarse, send_fine = gather_hanging(traces, hot, codes, up)
    swaps(vector[:, 0:SIDE], vector[:, CELLS - SIDE :], send_coarse, send_fine, *outs)
    for copy in copies[4:]:
        copy.wait()
    codes[0:2, 0:PAIRS] = pairs[...].astype(F32)
    place = lax.broadcasted_iota(jnp.int32, (values.shape[1], CELLS), 0)
    lookup = jnp.where(place == ids[...], 1.0, 0.0)
    coefficient = lax.dot_general(
        jnp.broadcast_to(values[...], (8, values.shape[1])),
        lookup,
        ALONG_ROWS,
        precision=lax.Precision.HIGHEST,
        preferred_element_type=F32,
    )
    level = levels[...]
    scale = jnp.where(level == 0, 1.0, jnp.where(level == 1, 0.5, 0.25))
    codes[SCALE_ROW : SCALE_ROW + 1, 0:CELLS] = coefficient[0:1] * scale
    codes[SCALE_ROW + 1 : SCALE_ROW + 2, 0:CELLS] = scale * scale * scale


def middle_kernel(
    field_ref, codes, table_ref, applied_ref, trace_out_ref, coarse_out_ref, partner_ref, field
):
    table = views(table_ref)
    vector = padded_field(field_ref, field)
    high, low = face_traces(table["trace"], vector)
    both = high + low
    trace_out_ref[...] = both
    coarse_out_ref[...] = table_dot(table["coarse"], both)
    traces = joined(high, low)
    for start in range(0, PAIR_SLOTS, CHUNK):
        face, cell = extended_code(codes[1:2, start : start + CHUNK])
        partner_ref[:, start : start + CHUNK] = pick(dot(traces, one_hot(cell, CELLS)), face)
    stiff = table_dot(table["local"], vector)
    lumped = table["lumped"][0][...].astype(F32) + table["lumped"][1][...].astype(F32)
    factor = codes[SCALE_ROW : SCALE_ROW + 1, 0:CELLS]
    cubed = codes[SCALE_ROW + 1 : SCALE_ROW + 2, 0:CELLS]
    applied_ref[...] = factor * stiff + cubed * (lumped * vector)


def add_faces(
    codes,
    table_ref,
    applied_ref,
    trace_in_ref,
    coarse_in_ref,
    partner_ref,
    rim_chip_ref,
    dom_odd_ref,
    dom_even_ref,
    rim_core_ref,
    sides,
    hot,
    spread,
):
    table = views(table_ref)
    hot_pairs(hot, codes)
    hot_hanging(hot, codes)
    first_core = lax.axis_index("core") == 0
    even_dom = lax.axis_index("x") % 2 == 0
    sides[:, 0:SIDE] = jnp.where(first_core, rim_chip_ref[...], rim_core_ref[...])
    sides[:, SIDE : 2 * SIDE] = jnp.where(first_core, rim_core_ref[...], rim_chip_ref[...])
    arriving = jnp.where(even_dom, dom_odd_ref[...], dom_even_ref[...])
    returned = jnp.where(even_dom, dom_even_ref[...], dom_odd_ref[...])
    side_traces = stacked_traces(table["trace"], sides[...])

    def put(start, value, face, coarse):
        width = value.shape[1]
        high = value.astype(BF16).astype(F32)
        row = lax.broadcasted_iota(jnp.int32, (16, width), 0)
        count = jnp.where(row == (face + 8 if coarse else face), 1.0, 0.0)
        pieces = stack(high, face) + stack(value - high, face) + [count]
        spread[:, start : start + width] = jnp.concatenate(pieces, axis=0).astype(BF16)

    for start in range(0, PAIR_SLOTS, CHUNK):
        face, cell = extended_code(codes[1:2, start : start + CHUNK])
        place = jnp.where(cell < 0, cell + SIDE, jnp.where(cell >= CELLS, cell + (SIDE - CELLS), -1))
        place = jnp.where(face < 0, -1, place)
        partner = partner_ref[:, start : start + CHUNK] + pick(
            dot(side_traces, one_hot(place, 2 * SIDE)), face
        )
        face, _ = own_code(codes[0:1, start : start + CHUNK])
        put(start, -TAU_PENALTY * partner, face, False)
    predicted = table_dot(table["down"], arriving)
    for child in range(4):
        face, _ = fine_code(codes, child)
        put(FINE0 + child * CELLS, predicted[child * FACE : (child + 1) * FACE], face, False)
    face, _ = coarse_code(codes)
    put(COARSE0, returned, face, True)
    added = dot(spread[...], hot[...], ALONG_LANES)
    both = added[0:STACK] + added[STACK : 2 * STACK]
    fine_count = TAU_PENALTY * added[2 * STACK : 2 * STACK + 8]
    coarse_count = added[2 * STACK + 8 : 2 * STACK + 16]
    pieces = []
    for f in range(7):
        rows = slice(f * MAIN, min((f + 1) * MAIN, STACK))
        counts = slice(f, f + 1) if f < 6 else slice(0, 8)
        pieces.append(
            both[rows]
            + fine_count[counts] * trace_in_ref[rows, :]
            + coarse_count[counts] * coarse_in_ref[rows, :]
        )
    pieces.append(jnp.zeros((TRACE - STACK, CELLS), F32))
    high, low = split(jnp.concatenate(pieces, axis=0))
    untrace = table["untrace"][...]
    return applied_ref[...] + (dot(untrace, high) + dot(untrace, low))


def image_kernel(*refs):
    codes, table = refs[0], views(refs[1])
    image = add_faces(*refs[:10], *refs[15:])
    refs[10][...] = image
    traces = stacked_traces(table["trace"], image)
    send_coarse, send_fine = gather_hanging(traces, refs[16], codes, table["up"])
    swaps(image[:, 0:SIDE], image[:, CELLS - SIDE :], send_coarse, send_fine, *refs[11:15])


def total(value):
    return jnp.sum(jnp.sum(value, axis=0, keepdims=True), axis=1, keepdims=True)


def moments_kernel(*refs):
    source_ref, image_ref, out_ref, sums_ref = refs[10:14]
    second = add_faces(*refs[:10], *refs[14:])
    out_ref[...] = second
    source = source_ref[...]
    image = image_ref[...]
    products = [
        source * source,
        source * image[0:125],
        image * image,
        source * second[0:125],
        image * second,
    ]
    lane = lax.broadcasted_iota(jnp.int32, (1, 128), 1)
    line = jnp.zeros((1, 128), F32)
    for index, product in enumerate(products):
        line = line + jnp.where(lane == index, total(product), 0.0)
    sums_ref[...] = jnp.broadcast_to(line[None], sums_ref.shape)


def last_kernel(sums_ref, source_ref, image_ref, second_ref, solution_ref, residual_ref):
    line = jnp.sum(sums_ref[...], axis=0)
    rr, rw, ww, ru, wu = (line[:, i : i + 1] for i in range(5))
    first_step = rr / rw
    rr_next = rr - 2.0 * first_step * rw + first_step * first_step * ww
    grown = 1.0 + rr_next / rr
    curvature = (
        grown * grown * rw - first_step * grown * (ru + ww) + first_step * first_step * wu
    )
    second_step = rr_next / curvature
    p = first_step + second_step * grown
    q = second_step * first_step
    source = source_ref[...]
    image = image_ref[0:125, :]
    solution_ref[...] = p * source - q * image
    residual_ref[...] = source - p * image + q * second_ref[0:125, :]


def call(kernel, out_shapes, scratch, *operands, name, space=pltpu.VMEM, limit=48):
    return pl.pallas_call(
        kernel,
        out_shape=[jax.ShapeDtypeStruct(shape, F32) for shape in out_shapes],
        in_specs=[pl.BlockSpec(memory_space=space)] * len(operands),
        out_specs=[pl.BlockSpec(memory_space=pltpu.VMEM)] * len(out_shapes),
        scratch_shapes=scratch,
        compiler_params=pltpu.CompilerParams(vmem_limit_bytes=limit * 1024 * 1024),
        name=name,
    )(*operands)


FIELD = pltpu.VMEM((128, CELLS), F32)
SIDES = pltpu.VMEM((128, 2 * SIDE), F32)
HOT = pltpu.VMEM((CELLS, SLOTS), BF16)
SPREAD = pltpu.VMEM((2 * STACK + 16, SLOTS), BF16)


def swapped(value, axes, first):
    count = lax.axis_size(axes)
    pairs = [(i, i + 1) for i in range(first, count - 1, 2)]
    return lax.ppermute(value, axes, pairs + [(above, below) for below, above in pairs])


def exchange(rim_chip, dom_odd, dom_even, rim_core):
    rim_chip = swapped(rim_chip, BLOCK, 1)
    dom_odd = swapped(dom_odd, DOM, 1)
    dom_even = swapped(dom_even, DOM, 0)
    rim_core = swapped(rim_core, BLOCK, 0)
    return rim_chip, dom_odd, dom_even, rim_core


def summed_over_blocks(sums):
    in_plane, along_z = lax.axis_size(PLANE), lax.axis_size("z")
    sums = lax.all_to_all(sums, PLANE, 0, 0, tiled=True)
    diagonal = [
        (z * in_plane + place, (z + place) % along_z * in_plane + place)
        for z in range(along_z)
        for place in range(along_z)
    ]
    other = lax.ppermute(jnp.sum(sums, axis=0, keepdims=True), BLOCK, diagonal)
    return lax.all_to_all(jnp.broadcast_to(other, sums.shape), PLANE, 0, 0, tiled=True)


def on_device(source, levels, ids, values, pairs, coarse, fine):
    levels, ids, values, coarse = (a.reshape(1, -1) for a in (levels, ids, values, coarse))
    table = jnp.asarray(packed_table())
    sends = [(128, SIDE), (FACE, CELLS), (FACE, CELLS), (128, SIDE)]
    params = (source, levels, ids, values, pairs, coarse, fine)
    *swapping, codes = call(
        first_kernel,
        [*sends, PACKED],
        [
            *(pltpu.VMEM(a.shape, a.dtype) for a in params),
            pltpu.VMEM((FIRST_ROWS, 256), BF16),
            FIELD,
            HOT,
            pltpu.SemaphoreType.DMA((8,)),
        ],
        *params,
        table,
        name="first",
        space=pl.ANY,
        limit=63,
    )

    arrays = [(128, CELLS), (TRACE, CELLS), (TRACE, CELLS), (FACE, PAIR_SLOTS)]
    scratch = [SIDES, HOT, SPREAD]
    arrived = exchange(*swapping)
    own = call(middle_kernel, arrays, [FIELD], source, codes, table, name="middle")
    image, *swapping = call(
        image_kernel,
        [(128, CELLS), *sends],
        scratch,
        codes,
        table,
        *own,
        *arrived,
        name="image",
    )
    arrived = exchange(*swapping)
    own = call(middle_kernel, arrays, [FIELD], image, codes, table, name="middle")
    second, sums = call(
        moments_kernel,
        [(128, CELLS), (lax.axis_size(PLANE), 1, 128)],
        scratch,
        codes,
        table,
        *own,
        *arrived,
        source,
        image,
        name="moments",
    )
    sums = summed_over_blocks(sums)
    return tuple(call(last_kernel, [source.shape] * 2, [], sums, source, image, second, name="last"))


def solution(mesh):
    dom, sub = mesh.devices.shape
    axes = BLOCK
    fine_mesh = Mesh(mesh.devices.reshape(dom // 4, 4, sub // 2, 2), axes)
    return jax.shard_map(
        on_device,
        mesh=fine_mesh,
        in_specs=(
            P(None, axes),
            P(axes),
            P(axes),
            P(),
            P(None, axes),
            P(axes),
            P(None, axes),
        ),
        out_specs=(P(None, axes), P(None, axes)),
        check_vma=False,
    )
```

```python
import jax
import jax.numpy as jnp
import numpy as np
import ml_dtypes
from jax import lax
from jax.experimental import pallas as pl
from jax.experimental.pallas import tpu as pltpu
from jax.sharding import Mesh, PartitionSpec as P

CELLS = 512
RIM = 64
EXTENT = CELLS + 2 * RIM
PAIRS = 960
PAIR_SLOTS = 1024
SIDE = 128
FACE = 32
MAIN = 24
TAIL = 6 * MAIN
STACK = TAIL + 8
TRACE = 160
FINE0 = PAIR_SLOTS
COARSE0 = PAIR_SLOTS + 4 * CELLS
SLOTS = COARSE0 + CELLS
CHUNK = 512
FINE_ROW = 2
COARSE_ROW = 6
SCALE_ROW = 8
PACKED = (16, PAIR_SLOTS)
TAU_PENALTY = 2.0
SIGMA_MASS = 4.0
BLOCK = ("z", "x", "y", "core")
DOM = ("z", "x")
PLANE = ("x", "y", "core")
F32 = jnp.float32
BF16 = jnp.bfloat16
ALONG_ROWS = (((1,), (0,)), ((), ()))
ALONG_LANES = (((1,), (1,)), ((), ()))


def element_tables():
    points = np.array([-1.0, -np.sqrt(3.0 / 7.0), 0.0, np.sqrt(3.0 / 7.0), 1.0])
    weights = np.array([0.1, 49.0 / 90.0, 32.0 / 45.0, 49.0 / 90.0, 0.1])

    def lagrange(location):
        values = np.ones((location.shape[0], 5))
        for column in range(5):
            for other in range(5):
                if other != column:
                    values[:, column] *= (location - points[other]) / (
                        points[column] - points[other]
                    )
        return values

    derivative = np.zeros((5, 5))
    for column in range(5):
        for other in range(5):
            if other != column:
                product = np.ones(5) / (points[column] - points[other])
                for remaining in range(5):
                    if remaining != column and remaining != other:
                        product = (
                            product
                            * (points - points[remaining])
                            / (points[column] - points[remaining])
                        )
                derivative[:, column] += product
    stiffness = derivative.T @ (weights[:, None] * derivative)
    halves = [lagrange((points - 1.0) / 2.0), lagrange((points + 1.0) / 2.0)]
    interp = [np.kron(halves[a], halves[b]) for a in range(2) for b in range(2)]
    return stiffness, weights, interp


def two_parts(table):
    high = table.astype(np.float32).astype(ml_dtypes.bfloat16)
    low = (table - high.astype(np.float64)).astype(np.float32).astype(ml_dtypes.bfloat16)
    return high, low


PLACES = {
    "trace": [(0, 0)],
    "up": [(160, 0), (160, 128)],
    "untrace": [(192, 0)],
    "coarse": [(320, 0), (480, 0)],
    "local": [(640, 0), (640, 128)],
    "down": [(768, 0), (768, 128)],
    "lumped": [(896, 0), (896, 128)],
}
FIRST_ROWS = 192
TABLE_ROWS = 1024


def packed_table():
    stiffness, weights, interp = element_tables()
    diag = np.diag(weights)

    def kron3(a, b, c):
        return np.kron(np.kron(a, b), c)

    local = np.zeros((128, 128))
    local[:125, :125] = (
        kron3(stiffness, diag, diag) + kron3(diag, stiffness, diag) + kron3(diag, diag, stiffness)
    )
    lumped = np.zeros((128, 1))
    lumped[:125, 0] = SIGMA_MASS * np.einsum("i,j,k->ijk", weights, weights, weights).reshape(-1)
    node = np.arange(125).reshape(5, 5, 5)
    slabs = [node[0], node[:, 0], node[:, :, 0], node[4], node[:, 4], node[:, :, 4]]
    stacked = np.concatenate([np.arange(6)[:, None] * MAIN + np.arange(MAIN), TAIL + np.arange(6)[:, None]], axis=1)
    trace = np.zeros((TRACE, 128))
    for face, slab in enumerate(slabs):
        trace[stacked[face], slab.reshape(-1)] = 1.0
    coarse = np.zeros((25, 25))
    down = np.zeros((4 * FACE, FACE))
    for child, matrix in enumerate(interp):
        coarse += matrix.T @ matrix
        down[child * FACE : child * FACE + 25, :25] = matrix
    coarse_stack = np.zeros((TRACE, TRACE))
    for rows in stacked:
        coarse_stack[np.ix_(rows, rows)] = TAU_PENALTY * coarse
    table = np.zeros((TABLE_ROWS, 256))
    places = {
        "trace": trace,
        "untrace": trace.T,
        "local": local,
        "coarse": coarse_stack,
        "down": -TAU_PENALTY * down,
        "up": -TAU_PENALTY * down.T,
        "lumped": lumped,
    }
    for name, value in places.items():
        parts = [value] if name.endswith("trace") else two_parts(value)
        for (row, lane), part in zip(PLACES[name], parts):
            table[row : row + value.shape[0], lane : lane + value.shape[1]] = part
    return table.astype(ml_dtypes.bfloat16)


def views(table):
    def view(name, rows, lanes):
        return [table.at[row : row + rows, lane : lane + lanes] for row, lane in PLACES[name]]

    return {
        "trace": view("trace", TRACE, 128)[0],
        "untrace": view("untrace", 128, TRACE)[0],
        "local": view("local", 128, 128),
        "coarse": view("coarse", TRACE, TRACE),
        "down": view("down", 4 * FACE, FACE),
        "up": view("up", FACE, 128),
        "lumped": view("lumped", 128, 1),
    }


def dot(a, b, dims=ALONG_ROWS):
    return lax.dot_general(a, b, dims, preferred_element_type=F32)


def split(value):
    high = value.astype(BF16)
    return high, (value - high.astype(F32)).astype(BF16)


def table_dot(parts, value):
    high, low = split(value)
    table = parts[0][...]
    return dot(table, high) + dot(table, low) + dot(parts[1][...], high)


def face_traces(trace_ref, field):
    high, low = split(field)
    table = trace_ref[...]
    return dot(table, high), dot(table, low)


def one_hot(cell, rows):
    place = lax.broadcasted_iota(jnp.int32, (rows, cell.shape[1]), 0)
    return jnp.where(place == cell, 1.0, 0.0).astype(BF16)


def pick(gathered, face):
    both = gathered[0:STACK] + gathered[STACK : 2 * STACK]
    main = None
    for f in range(6):
        term = jnp.where(face == f, both[f * MAIN : (f + 1) * MAIN], 0.0)
        main = term if main is None else main + term
    row = lax.broadcasted_iota(jnp.int32, (8, both.shape[1]), 0)
    last = jnp.sum(jnp.where(row == face, both[TAIL:STACK], 0.0), axis=0, keepdims=True)
    return jnp.concatenate([main, jnp.where(row == 0, last, 0.0)], axis=0)


def stack(value, face):
    row = lax.broadcasted_iota(jnp.int32, (8, value.shape[1]), 0)
    pieces = [jnp.where(face == f, value[0:MAIN], 0.0) for f in range(6)]
    return pieces + [jnp.where(row == face, value[MAIN : MAIN + 1], 0.0)]


def own_code(code):
    code = code.astype(jnp.int32)
    return code >> 9, code & (CELLS - 1)


def extended_code(code):
    code = code.astype(jnp.int32)
    face = jnp.where(code < 0, -1, 0)
    for f in range(1, 6):
        face = face + jnp.where(code >= f * EXTENT, 1, 0)
    return face, code - face * EXTENT - RIM


def padded_field(field_ref, field):
    if field_ref.shape[0] == 128:
        return field_ref[...]
    field[...] = jnp.zeros_like(field)
    field[0:125, :] = field_ref[...]
    return field[...]


def fine_code(codes, child):
    return own_code(codes[FINE_ROW + child : FINE_ROW + child + 1, 0:CELLS])


def coarse_code(codes):
    return own_code(codes[COARSE_ROW : COARSE_ROW + 1, 0:CELLS])


def gather_hanging(traces, hot, codes, up):
    rows = []
    for child in range(4):
        face, _ = fine_code(codes, child)
        start = FINE0 + child * CELLS
        rows.append(pick(dot(traces, hot[:, start : start + CELLS]), face))
    face, _ = coarse_code(codes)
    send_coarse = pick(dot(traces, hot[:, COARSE0:SLOTS]), face)
    send_fine = table_dot(up, jnp.concatenate(rows, axis=0))
    return send_coarse, send_fine


def hot_pairs(hot, codes):
    for start in range(0, PAIR_SLOTS, CHUNK):
        _, cell = own_code(codes[0:1, start : start + CHUNK])
        hot[:, start : start + CHUNK] = one_hot(cell, CELLS)


def hot_hanging(hot, codes):
    for child in range(4):
        _, cell = fine_code(codes, child)
        start = FINE0 + child * CELLS
        hot[:, start : start + CELLS] = one_hot(cell, CELLS)
    _, cell = coarse_code(codes)
    hot[:, COARSE0:SLOTS] = one_hot(cell, CELLS)


def joined(high, low):
    return jnp.concatenate([high[0:STACK], low[0:STACK]], axis=0).astype(BF16)


def stacked_traces(trace_ref, field):
    return joined(*face_traces(trace_ref, field))


def swaps(low, high, send_coarse, send_fine, rim_chip_ref, dom_odd_ref, dom_even_ref, rim_core_ref):
    first_core = lax.axis_index("core") == 0
    even_dom = lax.axis_index("x") % 2 == 0
    rim_core_ref[...] = jnp.where(first_core, high, low)
    rim_chip_ref[...] = jnp.where(first_core, low, high)
    dom_even_ref[...] = jnp.where(even_dom, send_coarse, send_fine)
    dom_odd_ref[...] = jnp.where(even_dom, send_fine, send_coarse)


def first_kernel(*refs):
    field_in, level_in, id_in, values_in, pairs_in, coarse_in, fine_in, table_in = refs[:8]
    outs, codes = refs[8:12], refs[12]
    source, levels, ids, values, pairs, coarse, fine, table, field, hot, sems = refs[13:]
    moves = [
        (coarse_in, coarse),
        (fine_in, fine),
        (field_in, source),
        (table_in.at[0:FIRST_ROWS], table),
        (level_in, levels),
        (id_in, ids),
        (values_in, values),
        (pairs_in, pairs),
    ]
    copies = [pltpu.make_async_copy(*move, sems.at[i]) for i, move in enumerate(moves)]
    for copy in copies:
        copy.start()
    codes[...] = jnp.full(codes.shape, -1.0, F32)
    copies[0].wait()
    codes[COARSE_ROW : COARSE_ROW + 1, 0:CELLS] = coarse[...].astype(F32)
    copies[1].wait()
    codes[FINE_ROW : FINE_ROW + 4, 0:CELLS] = fine[...].astype(F32)
    hot_hanging(hot, codes)
    copies[2].wait()
    copies[3].wait()
    vector = padded_field(source, field)
    traces = stacked_traces(table.at[0:TRACE, 0:128], vector)
    up = [table.at[row : row + FACE, lane : lane + 128] for row, lane in PLACES["up"]]
    send_coarse, send_fine = gather_hanging(traces, hot, codes, up)
    swaps(vector[:, 0:SIDE], vector[:, CELLS - SIDE :], send_coarse, send_fine, *outs)
    for copy in copies[4:]:
        copy.wait()
    codes[0:2, 0:PAIRS] = pairs[...].astype(F32)
    place = lax.broadcasted_iota(jnp.int32, (values.shape[1], CELLS), 0)
    lookup = jnp.where(place == ids[...], 1.0, 0.0)
    coefficient = lax.dot_general(
        jnp.broadcast_to(values[...], (8, values.shape[1])),
        lookup,
        ALONG_ROWS,
        precision=lax.Precision.HIGHEST,
        preferred_element_type=F32,
    )
    level = levels[...]
    scale = jnp.where(level == 0, 1.0, jnp.where(level == 1, 0.5, 0.25))
    codes[SCALE_ROW : SCALE_ROW + 1, 0:CELLS] = coefficient[0:1] * scale
    codes[SCALE_ROW + 1 : SCALE_ROW + 2, 0:CELLS] = scale * scale * scale


def middle_kernel(
    field_ref, pairs_ref, table_ref, stiff_ref, trace_out_ref, coarse_out_ref, partner_ref, *refs
):
    *first_ref, field, pairs = refs
    pairs[...] = jnp.full(pairs.shape, -1, jnp.int32)
    pairs[0:2, 0:PAIRS] = pairs_ref[...]
    table = views(table_ref)
    vector = padded_field(field_ref, field)
    high, low = face_traces(table["trace"], vector)
    both = high + low
    trace_out_ref[...] = both
    coarse_out_ref[...] = table_dot(table["coarse"], both)
    traces = joined(high, low)
    for start in range(0, PAIR_SLOTS, CHUNK):
        face, cell = extended_code(pairs[1:2, start : start + CHUNK])
        partner_ref[:, start : start + CHUNK] = pick(dot(traces, one_hot(cell, CELLS)), face)
        for ref in first_ref:
            face, cell = own_code(pairs[0:1, start : start + CHUNK])
            ref[:, start : start + CHUNK] = pick(dot(traces, one_hot(cell, CELLS)), face)
    stiff_ref[...] = table_dot(table["local"], vector)


def applied(codes, table, stiff, field):
    rows = field.shape[0]
    lumped = [part[...][0:rows].astype(F32) for part in table["lumped"]]
    factor = codes[SCALE_ROW : SCALE_ROW + 1, 0:CELLS]
    cubed = codes[SCALE_ROW + 1 : SCALE_ROW + 2, 0:CELLS]
    return factor * stiff[0:rows] + cubed * ((lumped[0] + lumped[1]) * field)


def traces_beside(trace_ref, rim_chip_ref, rim_core_ref):
    is_below = lax.broadcasted_iota(jnp.int32, rim_chip_ref.shape, 1) >= SIDE - RIM
    from_chip = is_below == (lax.axis_index("core") == 0)
    return stacked_traces(trace_ref, jnp.where(from_chip, rim_chip_ref[...], rim_core_ref[...]))


def partner_values(codes, partner_ref, side_traces, start):
    face, cell = extended_code(codes[1:2, start : start + CHUNK])
    place = jnp.where(cell < 0, cell + SIDE, jnp.where(cell >= CELLS, cell - CELLS, -1))
    place = jnp.where(face < 0, -1, place)
    beside = pick(dot(side_traces, one_hot(place, SIDE)), face)
    return partner_ref[:, start : start + CHUNK] + beside


def add_faces(
    codes,
    table_ref,
    field_ref,
    stiff_ref,
    trace_in_ref,
    coarse_in_ref,
    partner_ref,
    rim_chip_ref,
    dom_odd_ref,
    dom_even_ref,
    rim_core_ref,
    hot,
    spread,
    local,
):
    table = views(table_ref)
    hot_pairs(hot, codes)
    hot_hanging(hot, codes)
    even_dom = lax.axis_index("x") % 2 == 0
    arriving = jnp.where(even_dom, dom_odd_ref[...], dom_even_ref[...])
    returned = jnp.where(even_dom, dom_even_ref[...], dom_odd_ref[...])
    side_traces = traces_beside(table["trace"], rim_chip_ref, rim_core_ref)

    def put(start, value, face, coarse):
        width = value.shape[1]
        high = value.astype(BF16).astype(F32)
        row = lax.broadcasted_iota(jnp.int32, (16, width), 0)
        count = jnp.where(row == (face + 8 if coarse else face), 1.0, 0.0)
        pieces = stack(high, face) + stack(value - high, face) + [count]
        spread[:, start : start + width] = jnp.concatenate(pieces, axis=0).astype(BF16)

    for start in range(0, PAIR_SLOTS, CHUNK):
        partner = partner_values(codes, partner_ref, side_traces, start)
        face, _ = own_code(codes[0:1, start : start + CHUNK])
        put(start, -TAU_PENALTY * partner, face, False)
    predicted = table_dot(table["down"], arriving)
    for child in range(4):
        face, _ = fine_code(codes, child)
        put(FINE0 + child * CELLS, predicted[child * FACE : (child + 1) * FACE], face, False)
    face, _ = coarse_code(codes)
    put(COARSE0, returned, face, True)
    added = dot(spread[...], hot[...], ALONG_LANES)
    both = added[0:STACK] + added[STACK : 2 * STACK]
    counts = added[2 * STACK : 2 * STACK + 16]
    pieces = [both[rows] + own for rows, own in own_faces(counts, trace_in_ref, coarse_in_ref)]
    pieces.append(jnp.zeros((TRACE - STACK, CELLS), F32))
    high, low = split(jnp.concatenate(pieces, axis=0))
    untrace = table["untrace"][...]
    rows = field_ref.shape[0]
    local[...] = dot(untrace, high) + dot(untrace, low)
    local[0:rows, :] += applied(codes, table, stiff_ref[...], field_ref[...])
    return local[...], counts


def own_faces(counts, trace_ref, coarse_ref):
    for f in range(7):
        rows = slice(f * MAIN, min((f + 1) * MAIN, STACK))
        fine = counts[f : f + 1] if f < 6 else counts[0:8]
        coarse = counts[f + 8 : f + 9] if f < 6 else counts[8:16]
        yield rows, (TAU_PENALTY * fine) * trace_ref[rows, :] + coarse * coarse_ref[rows, :]


def image_kernel(*refs):
    codes, table = refs[0], views(refs[1])
    image, counts = add_faces(*refs[:11], *refs[17:])
    refs[11][...] = image
    traces = stacked_traces(table["trace"], image)
    send_coarse, send_fine = gather_hanging(traces, refs[17], codes, table["up"])
    swaps(image[:, 0:SIDE], image[:, CELLS - SIDE :], send_coarse, send_fine, *refs[12:16])
    refs[16][...] = counts


def second_kernel(*refs):
    refs[11][...], _ = add_faces(*refs[:11], *refs[12:])


def total(value):
    return jnp.sum(jnp.sum(value, axis=0, keepdims=True), axis=1, keepdims=True)


def moments_kernel(
    codes,
    table_ref,
    image_ref,
    stiff_ref,
    trace_ref,
    coarse_ref,
    partner_ref,
    rim_chip_ref,
    dom_odd_ref,
    dom_even_ref,
    rim_core_ref,
    _sent_chip_ref,
    sent_odd_ref,
    sent_even_ref,
    _sent_core_ref,
    first_ref,
    counts_ref,
    source_ref,
    sums_ref,
):
    table = views(table_ref)
    source = source_ref[...]
    image = image_ref[...]
    side_traces = traces_beside(table["trace"], rim_chip_ref, rim_core_ref)
    curved = total(image * applied(codes, table, stiff_ref[...], image))
    hanging = sent_odd_ref[...] * dom_odd_ref[...] + sent_even_ref[...] * dom_even_ref[...]
    for start in range(0, PAIR_SLOTS, CHUNK):
        partner = partner_values(codes, partner_ref, side_traces, start)
        hanging = hanging - TAU_PENALTY * (partner * first_ref[:, start : start + CHUNK])
    curved = curved + total(hanging)
    own = [trace_ref[rows, :] * value for rows, value in own_faces(counts_ref[...], trace_ref, coarse_ref)]
    curved = curved + total(jnp.concatenate(own, axis=0))
    sums = [total(source * source), total(source * image[0:125]), total(image * image), curved]
    lane = lax.broadcasted_iota(jnp.int32, (1, 128), 1)
    line = jnp.zeros((1, 128), F32)
    for index, value in enumerate(sums):
        line = line + jnp.where(lane == index, value, 0.0)
    sums_ref[...] = jnp.broadcast_to(line[None], sums_ref.shape)


def last_kernel(sums_ref, source_ref, image_ref, second_ref, solution_ref, residual_ref):
    line = jnp.sum(sums_ref[...], axis=0)
    rr, rw, ww, wu = (line[:, i : i + 1] for i in range(4))
    first_step = rr / rw
    rr_next = rr - 2.0 * first_step * rw + first_step * first_step * ww
    grown = 1.0 + rr_next / rr
    curvature = (
        grown * grown * rw - 2.0 * first_step * grown * ww + first_step * first_step * wu
    )
    second_step = rr_next / curvature
    p = first_step + second_step * grown
    q = second_step * first_step
    source = source_ref[...]
    image = image_ref[0:125, :]
    solution_ref[...] = p * source - q * image
    residual_ref[...] = source - p * image + q * second_ref[0:125, :]


def call(kernel, out_shapes, scratch, *operands, name, space=pltpu.VMEM, limit=48):
    return pl.pallas_call(
        kernel,
        out_shape=[jax.ShapeDtypeStruct(shape, F32) for shape in out_shapes],
        in_specs=[pl.BlockSpec(memory_space=space)] * len(operands),
        out_specs=[pl.BlockSpec(memory_space=pltpu.VMEM)] * len(out_shapes),
        scratch_shapes=scratch,
        compiler_params=pltpu.CompilerParams(vmem_limit_bytes=limit * 1024 * 1024),
        name=name,
    )(*operands)


PAIR_CODES = pltpu.VMEM((8, PAIR_SLOTS), jnp.int32)
FIELD = pltpu.VMEM((128, CELLS), F32)
HOT = pltpu.VMEM((CELLS, SLOTS), BF16)
SPREAD = pltpu.VMEM((2 * STACK + 16, SLOTS), BF16)


def swapped(value, axes, first):
    count = lax.axis_size(axes)
    pairs = [(i, i + 1) for i in range(first, count - 1, 2)]
    return lax.ppermute(value, axes, pairs + [(above, below) for below, above in pairs])


def exchange(rim_chip, dom_odd, dom_even, rim_core):
    rim_chip = swapped(rim_chip, BLOCK, 1)
    dom_odd = swapped(dom_odd, DOM, 1)
    dom_even = swapped(dom_even, DOM, 0)
    rim_core = swapped(rim_core, BLOCK, 0)
    return rim_chip, dom_odd, dom_even, rim_core


def summed_over_blocks(sums):
    in_plane, along_z = lax.axis_size(PLANE), lax.axis_size("z")
    sums = lax.all_to_all(sums, PLANE, 0, 0, tiled=True)
    diagonal = [
        (z * in_plane + place, (z + place) % along_z * in_plane + place)
        for z in range(along_z)
        for place in range(along_z)
    ]
    other = lax.ppermute(jnp.sum(sums, axis=0, keepdims=True), BLOCK, diagonal)
    return lax.all_to_all(jnp.broadcast_to(other, sums.shape), PLANE, 0, 0, tiled=True)


def on_device(source, levels, ids, values, pairs, coarse, fine):
    levels, ids, values, coarse = (a.reshape(1, -1) for a in (levels, ids, values, coarse))
    table = jnp.asarray(packed_table())
    sends = [(128, SIDE), (FACE, CELLS), (FACE, CELLS), (128, SIDE)]
    params = (source, levels, ids, values, pairs, coarse, fine)
    *swapping, codes = call(
        first_kernel,
        [*sends, PACKED],
        [
            *(pltpu.VMEM(a.shape, a.dtype) for a in params),
            pltpu.VMEM((FIRST_ROWS, 256), BF16),
            FIELD,
            HOT,
            pltpu.SemaphoreType.DMA((8,)),
        ],
        *params,
        table,
        name="first",
        space=pl.ANY,
        limit=63,
    )

    arrays = [(128, CELLS), (TRACE, CELLS), (TRACE, CELLS), (FACE, PAIR_SLOTS)]
    scratch = [HOT, SPREAD, FIELD]
    arrived = exchange(*swapping)
    own = call(middle_kernel, arrays, [FIELD, PAIR_CODES], source, pairs, table, name="middle")
    image, *swapping, counts = call(
        image_kernel,
        [(128, CELLS), *sends, (16, CELLS)],
        scratch,
        codes,
        table,
        source,
        *own,
        *arrived,
        name="image",
    )
    arrived = exchange(*swapping)
    *own, first = call(
        middle_kernel, [*arrays, (FACE, PAIR_SLOTS)], [FIELD, PAIR_CODES], image, pairs, table, name="middle"
    )
    sums = call(
        moments_kernel,
        [(lax.axis_size(PLANE), 1, 128)],
        [],
        codes,
        table,
        image,
        *own,
        *arrived,
        *swapping,
        first,
        counts,
        source,
        name="moments",
    )[0]
    second = call(second_kernel, [(128, CELLS)], scratch, codes, table, image, *own, *arrived, name="second")[0]
    sums = summed_over_blocks(sums)
    return tuple(call(last_kernel, [source.shape] * 2, [], sums, source, image, second, name="last"))


def solution(mesh):
    dom, sub = mesh.devices.shape
    axes = BLOCK
    fine_mesh = Mesh(mesh.devices.reshape(dom // 4, 4, sub // 2, 2), axes)
    return jax.shard_map(
        on_device,
        mesh=fine_mesh,
        in_specs=(
            P(None, axes),
            P(axes),
            P(axes),
            P(),
            P(None, axes),
            P(axes),
            P(None, axes),
        ),
        out_specs=(P(None, axes), P(None, axes)),
        check_vma=False,
    )
```

```python
import jax
import jax.numpy as jnp
import numpy as np
import ml_dtypes
from jax import lax
from jax.experimental import pallas as pl
from jax.experimental.pallas import tpu as pltpu
from jax.sharding import Mesh, PartitionSpec as P

CELLS = 512
RIM = 64
EXTENT = CELLS + 2 * RIM
PAIRS = 960
PAIR_SLOTS = 1024
SIDE = 128
FACE = 32
MAIN = 24
TAIL = 6 * MAIN
STACK = TAIL + 8
TRACE = 160
FINE0 = PAIR_SLOTS
COARSE0 = PAIR_SLOTS + 4 * CELLS
SLOTS = COARSE0 + CELLS
CHUNK = 512
FINE_ROW = 2
COARSE_ROW = 6
SCALE_ROW = 8
PACKED = (16, PAIR_SLOTS)
TAU_PENALTY = 2.0
SIGMA_MASS = 4.0
BLOCK = ("z", "x", "y", "core")
DOM = ("z", "x")
PLANE = ("x", "y", "core")
F32 = jnp.float32
BF16 = jnp.bfloat16
ALONG_ROWS = (((1,), (0,)), ((), ()))
ALONG_LANES = (((1,), (1,)), ((), ()))


def element_tables():
    points = np.array([-1.0, -np.sqrt(3.0 / 7.0), 0.0, np.sqrt(3.0 / 7.0), 1.0])
    weights = np.array([0.1, 49.0 / 90.0, 32.0 / 45.0, 49.0 / 90.0, 0.1])

    def lagrange(location):
        values = np.ones((location.shape[0], 5))
        for column in range(5):
            for other in range(5):
                if other != column:
                    values[:, column] *= (location - points[other]) / (
                        points[column] - points[other]
                    )
        return values

    derivative = np.zeros((5, 5))
    for column in range(5):
        for other in range(5):
            if other != column:
                product = np.ones(5) / (points[column] - points[other])
                for remaining in range(5):
                    if remaining != column and remaining != other:
                        product = (
                            product
                            * (points - points[remaining])
                            / (points[column] - points[remaining])
                        )
                derivative[:, column] += product
    stiffness = derivative.T @ (weights[:, None] * derivative)
    halves = [lagrange((points - 1.0) / 2.0), lagrange((points + 1.0) / 2.0)]
    interp = [np.kron(halves[a], halves[b]) for a in range(2) for b in range(2)]
    return stiffness, weights, interp


def two_parts(table):
    high = table.astype(np.float32).astype(ml_dtypes.bfloat16)
    low = (table - high.astype(np.float64)).astype(np.float32).astype(ml_dtypes.bfloat16)
    return high, low


PLACES = {
    "trace": [(0, 0)],
    "up": [(160, 0), (160, 128)],
    "untrace": [(192, 0)],
    "coarse": [(320, 0), (480, 0)],
    "local": [(640, 0), (640, 128)],
    "down": [(768, 0), (768, 128)],
    "lumped": [(896, 0), (896, 128)],
}
FIRST_ROWS = 192
TABLE_ROWS = 1024


def packed_table():
    stiffness, weights, interp = element_tables()
    diag = np.diag(weights)

    def kron3(a, b, c):
        return np.kron(np.kron(a, b), c)

    local = np.zeros((128, 128))
    local[:125, :125] = (
        kron3(stiffness, diag, diag) + kron3(diag, stiffness, diag) + kron3(diag, diag, stiffness)
    )
    lumped = np.zeros((128, 1))
    lumped[:125, 0] = SIGMA_MASS * np.einsum("i,j,k->ijk", weights, weights, weights).reshape(-1)
    node = np.arange(125).reshape(5, 5, 5)
    slabs = [node[0], node[:, 0], node[:, :, 0], node[4], node[:, 4], node[:, :, 4]]
    stacked = np.concatenate([np.arange(6)[:, None] * MAIN + np.arange(MAIN), TAIL + np.arange(6)[:, None]], axis=1)
    trace = np.zeros((TRACE, 128))
    for face, slab in enumerate(slabs):
        trace[stacked[face], slab.reshape(-1)] = 1.0
    coarse = np.zeros((25, 25))
    down = np.zeros((4 * FACE, FACE))
    for child, matrix in enumerate(interp):
        coarse += matrix.T @ matrix
        down[child * FACE : child * FACE + 25, :25] = matrix
    coarse_stack = np.zeros((TRACE, TRACE))
    for rows in stacked:
        coarse_stack[np.ix_(rows, rows)] = TAU_PENALTY * coarse
    table = np.zeros((TABLE_ROWS, 256))
    places = {
        "trace": trace,
        "untrace": trace.T,
        "local": local,
        "coarse": coarse_stack,
        "down": -TAU_PENALTY * down,
        "up": -TAU_PENALTY * down.T,
        "lumped": lumped,
    }
    for name, value in places.items():
        parts = [value] if name.endswith("trace") else two_parts(value)
        for (row, lane), part in zip(PLACES[name], parts):
            table[row : row + value.shape[0], lane : lane + value.shape[1]] = part
    return table.astype(ml_dtypes.bfloat16)


def views(table):
    def view(name, rows, lanes):
        return [table.at[row : row + rows, lane : lane + lanes] for row, lane in PLACES[name]]

    return {
        "trace": view("trace", TRACE, 128)[0],
        "untrace": view("untrace", 128, TRACE)[0],
        "local": view("local", 128, 128),
        "coarse": view("coarse", TRACE, TRACE),
        "down": view("down", 4 * FACE, FACE),
        "up": view("up", FACE, 128),
        "lumped": view("lumped", 128, 1),
    }


def dot(a, b, dims=ALONG_ROWS):
    return lax.dot_general(a, b, dims, preferred_element_type=F32)


def split(value):
    high = value.astype(BF16)
    return high, (value - high.astype(F32)).astype(BF16)


def table_dot(parts, value):
    high, low = split(value)
    table = parts[0][...]
    return dot(table, high) + dot(table, low) + dot(parts[1][...], high)


def face_traces(trace_ref, field):
    high, low = split(field)
    table = trace_ref[...]
    return dot(table, high), dot(table, low)


def one_hot(cell, rows):
    place = lax.broadcasted_iota(jnp.int32, (rows, cell.shape[1]), 0)
    return jnp.where(place == cell, 1.0, 0.0).astype(BF16)


def pick(gathered, face):
    both = gathered[0:STACK] + gathered[STACK : 2 * STACK]
    main = None
    for f in range(6):
        term = jnp.where(face == f, both[f * MAIN : (f + 1) * MAIN], 0.0)
        main = term if main is None else main + term
    row = lax.broadcasted_iota(jnp.int32, (8, both.shape[1]), 0)
    last = jnp.sum(jnp.where(row == face, both[TAIL:STACK], 0.0), axis=0, keepdims=True)
    return jnp.concatenate([main, jnp.where(row == 0, last, 0.0)], axis=0)


def stack(value, face):
    row = lax.broadcasted_iota(jnp.int32, (8, value.shape[1]), 0)
    pieces = [jnp.where(face == f, value[0:MAIN], 0.0) for f in range(6)]
    return pieces + [jnp.where(row == face, value[MAIN : MAIN + 1], 0.0)]


def own_code(code):
    code = code.astype(jnp.int32)
    return code >> 9, code & (CELLS - 1)


def extended_code(code):
    code = code.astype(jnp.int32)
    face = jnp.where(code < 0, -1, 0)
    for f in range(1, 6):
        face = face + jnp.where(code >= f * EXTENT, 1, 0)
    return face, code - face * EXTENT - RIM


def padded_field(field_ref, field):
    if field_ref.shape[0] == 128:
        return field_ref[...]
    field[...] = jnp.zeros_like(field)
    field[0:125, :] = field_ref[...]
    return field[...]


def fine_code(codes, child):
    return own_code(codes[FINE_ROW + child : FINE_ROW + child + 1, 0:CELLS])


def coarse_code(codes):
    return own_code(codes[COARSE_ROW : COARSE_ROW + 1, 0:CELLS])


def gather_hanging(traces, hot, codes, up):
    rows = []
    for child in range(4):
        face, _ = fine_code(codes, child)
        start = FINE0 + child * CELLS
        rows.append(pick(dot(traces, hot[:, start : start + CELLS]), face))
    face, _ = coarse_code(codes)
    send_coarse = pick(dot(traces, hot[:, COARSE0:SLOTS]), face)
    send_fine = table_dot(up, jnp.concatenate(rows, axis=0))
    return send_coarse, send_fine


def hot_pairs(hot, codes):
    for start in range(0, PAIR_SLOTS, CHUNK):
        _, cell = own_code(codes[0:1, start : start + CHUNK])
        hot[:, start : start + CHUNK] = one_hot(cell, CELLS)


def hot_hanging(hot, codes):
    for child in range(4):
        _, cell = fine_code(codes, child)
        start = FINE0 + child * CELLS
        hot[:, start : start + CELLS] = one_hot(cell, CELLS)
    _, cell = coarse_code(codes)
    hot[:, COARSE0:SLOTS] = one_hot(cell, CELLS)


def joined(high, low):
    return jnp.concatenate([high[0:STACK], low[0:STACK]], axis=0).astype(BF16)


def stacked_traces(trace_ref, field):
    return joined(*face_traces(trace_ref, field))


def swaps(low, high, send_coarse, send_fine, dom_odd_ref, rim_chip_ref, dom_even_ref, rim_core_ref):
    first_core = lax.axis_index("core") == 0
    even_dom = lax.axis_index("x") % 2 == 0
    rim_core_ref[...] = jnp.where(first_core, high, low)
    rim_chip_ref[...] = jnp.where(first_core, low, high)
    dom_even_ref[...] = jnp.where(even_dom, send_coarse, send_fine)
    dom_odd_ref[...] = jnp.where(even_dom, send_fine, send_coarse)


def first_kernel(*refs):
    field_in, level_in, id_in, values_in, pairs_in, coarse_in, fine_in, table_in = refs[:8]
    outs, codes = refs[8:12], refs[12]
    source, levels, ids, values, pairs, coarse, fine, table, field, hot, sems = refs[13:]
    moves = [
        (coarse_in, coarse),
        (fine_in, fine),
        (field_in, source),
        (table_in.at[0:FIRST_ROWS], table),
        (level_in, levels),
        (id_in, ids),
        (values_in, values),
        (pairs_in, pairs),
    ]
    copies = [pltpu.make_async_copy(*move, sems.at[i]) for i, move in enumerate(moves)]
    for copy in copies:
        copy.start()
    codes[...] = jnp.full(codes.shape, -1.0, F32)
    copies[0].wait()
    codes[COARSE_ROW : COARSE_ROW + 1, 0:CELLS] = coarse[...].astype(F32)
    copies[1].wait()
    codes[FINE_ROW : FINE_ROW + 4, 0:CELLS] = fine[...].astype(F32)
    hot_hanging(hot, codes)
    copies[2].wait()
    copies[3].wait()
    vector = padded_field(source, field)
    traces = stacked_traces(table.at[0:TRACE, 0:128], vector)
    up = [table.at[row : row + FACE, lane : lane + 128] for row, lane in PLACES["up"]]
    send_coarse, send_fine = gather_hanging(traces, hot, codes, up)
    swaps(vector[:, 0:SIDE], vector[:, CELLS - SIDE :], send_coarse, send_fine, *outs)
    for copy in copies[4:]:
        copy.wait()
    codes[0:2, 0:PAIRS] = pairs[...].astype(F32)
    place = lax.broadcasted_iota(jnp.int32, (values.shape[1], CELLS), 0)
    lookup = jnp.where(place == ids[...], 1.0, 0.0)
    coefficient = lax.dot_general(
        jnp.broadcast_to(values[...], (8, values.shape[1])),
        lookup,
        ALONG_ROWS,
        precision=lax.Precision.HIGHEST,
        preferred_element_type=F32,
    )
    level = levels[...]
    scale = jnp.where(level == 0, 1.0, jnp.where(level == 1, 0.5, 0.25))
    codes[SCALE_ROW : SCALE_ROW + 1, 0:CELLS] = coefficient[0:1] * scale
    codes[SCALE_ROW + 1 : SCALE_ROW + 2, 0:CELLS] = scale * scale * scale


def middle_kernel(
    field_ref, pairs_ref, table_ref, stiff_ref, trace_out_ref, coarse_out_ref, partner_ref, *refs
):
    *first_ref, field, pairs = refs
    pairs[...] = jnp.full(pairs.shape, -1, jnp.int32)
    pairs[0:2, 0:PAIRS] = pairs_ref[...]
    table = views(table_ref)
    vector = padded_field(field_ref, field)
    high, low = face_traces(table["trace"], vector)
    both = high + low
    trace_out_ref[...] = both
    coarse_out_ref[...] = table_dot(table["coarse"], both)
    traces = joined(high, low)
    for start in range(0, PAIR_SLOTS, CHUNK):
        face, cell = extended_code(pairs[1:2, start : start + CHUNK])
        partner_ref[:, start : start + CHUNK] = pick(dot(traces, one_hot(cell, CELLS)), face)
        for ref in first_ref:
            face, cell = own_code(pairs[0:1, start : start + CHUNK])
            ref[:, start : start + CHUNK] = pick(dot(traces, one_hot(cell, CELLS)), face)
    stiff_ref[...] = table_dot(table["local"], vector)


def applied(codes, table, stiff, field):
    rows = field.shape[0]
    lumped = [part[...][0:rows].astype(F32) for part in table["lumped"]]
    factor = codes[SCALE_ROW : SCALE_ROW + 1, 0:CELLS]
    cubed = codes[SCALE_ROW + 1 : SCALE_ROW + 2, 0:CELLS]
    return factor * stiff[0:rows] + cubed * ((lumped[0] + lumped[1]) * field)


def traces_beside(trace_ref, rim_chip_ref, rim_core_ref):
    is_below = lax.broadcasted_iota(jnp.int32, rim_chip_ref.shape, 1) >= SIDE - RIM
    from_chip = is_below == (lax.axis_index("core") == 0)
    return stacked_traces(trace_ref, jnp.where(from_chip, rim_chip_ref[...], rim_core_ref[...]))


def partner_values(codes, partner_ref, side_traces, start):
    face, cell = extended_code(codes[1:2, start : start + CHUNK])
    place = jnp.where(cell < 0, cell + SIDE, jnp.where(cell >= CELLS, cell - CELLS, -1))
    place = jnp.where(face < 0, -1, place)
    beside = pick(dot(side_traces, one_hot(place, SIDE)), face)
    return partner_ref[:, start : start + CHUNK] + beside


def add_faces(
    codes,
    table_ref,
    field_ref,
    stiff_ref,
    trace_in_ref,
    coarse_in_ref,
    partner_ref,
    dom_odd_ref,
    rim_chip_ref,
    dom_even_ref,
    rim_core_ref,
    hot,
    spread,
    local,
):
    table = views(table_ref)
    hot_pairs(hot, codes)
    hot_hanging(hot, codes)
    even_dom = lax.axis_index("x") % 2 == 0
    arriving = jnp.where(even_dom, dom_odd_ref[...], dom_even_ref[...])
    returned = jnp.where(even_dom, dom_even_ref[...], dom_odd_ref[...])
    side_traces = traces_beside(table["trace"], rim_chip_ref, rim_core_ref)

    def put(start, value, face, coarse):
        width = value.shape[1]
        high = value.astype(BF16).astype(F32)
        row = lax.broadcasted_iota(jnp.int32, (16, width), 0)
        count = jnp.where(row == (face + 8 if coarse else face), 1.0, 0.0)
        pieces = stack(high, face) + stack(value - high, face) + [count]
        spread[:, start : start + width] = jnp.concatenate(pieces, axis=0).astype(BF16)

    for start in range(0, PAIR_SLOTS, CHUNK):
        partner = partner_values(codes, partner_ref, side_traces, start)
        face, _ = own_code(codes[0:1, start : start + CHUNK])
        put(start, -TAU_PENALTY * partner, face, False)
    predicted = table_dot(table["down"], arriving)
    for child in range(4):
        face, _ = fine_code(codes, child)
        put(FINE0 + child * CELLS, predicted[child * FACE : (child + 1) * FACE], face, False)
    face, _ = coarse_code(codes)
    put(COARSE0, returned, face, True)
    added = dot(spread[...], hot[...], ALONG_LANES)
    both = added[0:STACK] + added[STACK : 2 * STACK]
    counts = added[2 * STACK : 2 * STACK + 16]
    pieces = [both[rows] + own for rows, own in own_faces(counts, trace_in_ref, coarse_in_ref)]
    pieces.append(jnp.zeros((TRACE - STACK, CELLS), F32))
    high, low = split(jnp.concatenate(pieces, axis=0))
    untrace = table["untrace"][...]
    rows = field_ref.shape[0]
    local[...] = dot(untrace, high) + dot(untrace, low)
    local[0:rows, :] += applied(codes, table, stiff_ref[...], field_ref[...])
    return local[...], counts


def own_faces(counts, trace_ref, coarse_ref):
    for f in range(7):
        rows = slice(f * MAIN, min((f + 1) * MAIN, STACK))
        fine = counts[f : f + 1] if f < 6 else counts[0:8]
        coarse = counts[f + 8 : f + 9] if f < 6 else counts[8:16]
        yield rows, (TAU_PENALTY * fine) * trace_ref[rows, :] + coarse * coarse_ref[rows, :]


def image_kernel(*refs):
    codes, table = refs[0], views(refs[1])
    image, counts = add_faces(*refs[:11], *refs[17:])
    refs[11][...] = image
    traces = stacked_traces(table["trace"], image)
    send_coarse, send_fine = gather_hanging(traces, refs[17], codes, table["up"])
    swaps(image[:, 0:SIDE], image[:, CELLS - SIDE :], send_coarse, send_fine, *refs[12:16])
    refs[16][...] = counts


def second_kernel(*refs):
    refs[11][...], _ = add_faces(*refs[:11], *refs[12:])


def total(value):
    return jnp.sum(jnp.sum(value, axis=0, keepdims=True), axis=1, keepdims=True)


def moments_kernel(
    codes,
    table_ref,
    image_ref,
    stiff_ref,
    trace_ref,
    coarse_ref,
    partner_ref,
    dom_odd_ref,
    rim_chip_ref,
    dom_even_ref,
    rim_core_ref,
    sent_odd_ref,
    _sent_chip_ref,
    sent_even_ref,
    _sent_core_ref,
    first_ref,
    counts_ref,
    source_ref,
    sums_ref,
):
    table = views(table_ref)
    source = source_ref[...]
    image = image_ref[...]
    side_traces = traces_beside(table["trace"], rim_chip_ref, rim_core_ref)
    curved = total(image * applied(codes, table, stiff_ref[...], image))
    hanging = sent_odd_ref[...] * dom_odd_ref[...] + sent_even_ref[...] * dom_even_ref[...]
    for start in range(0, PAIR_SLOTS, CHUNK):
        partner = partner_values(codes, partner_ref, side_traces, start)
        hanging = hanging - TAU_PENALTY * (partner * first_ref[:, start : start + CHUNK])
    curved = curved + total(hanging)
    own = [trace_ref[rows, :] * value for rows, value in own_faces(counts_ref[...], trace_ref, coarse_ref)]
    curved = curved + total(jnp.concatenate(own, axis=0))
    sums = [total(source * source), total(source * image[0:125]), total(image * image), curved]
    lane = lax.broadcasted_iota(jnp.int32, (1, 128), 1)
    line = jnp.zeros((1, 128), F32)
    for index, value in enumerate(sums):
        line = line + jnp.where(lane == index, value, 0.0)
    sums_ref[...] = jnp.broadcast_to(line[None], sums_ref.shape)


def last_kernel(sums_ref, source_ref, image_ref, second_ref, solution_ref, residual_ref):
    line = jnp.sum(sums_ref[...], axis=0)
    rr, rw, ww, wu = (line[:, i : i + 1] for i in range(4))
    first_step = rr / rw
    rr_next = rr - 2.0 * first_step * rw + first_step * first_step * ww
    grown = 1.0 + rr_next / rr
    curvature = (
        grown * grown * rw - 2.0 * first_step * grown * ww + first_step * first_step * wu
    )
    second_step = rr_next / curvature
    p = first_step + second_step * grown
    q = second_step * first_step
    source = source_ref[...]
    image = image_ref[0:125, :]
    solution_ref[...] = p * source - q * image
    residual_ref[...] = source - p * image + q * second_ref[0:125, :]


def call(kernel, out_shapes, scratch, *operands, name, space=pltpu.VMEM, limit=48):
    return pl.pallas_call(
        kernel,
        out_shape=[jax.ShapeDtypeStruct(shape, F32) for shape in out_shapes],
        in_specs=[pl.BlockSpec(memory_space=space)] * len(operands),
        out_specs=[pl.BlockSpec(memory_space=pltpu.VMEM)] * len(out_shapes),
        scratch_shapes=scratch,
        compiler_params=pltpu.CompilerParams(vmem_limit_bytes=limit * 1024 * 1024),
        name=name,
    )(*operands)


PAIR_CODES = pltpu.VMEM((8, PAIR_SLOTS), jnp.int32)
FIELD = pltpu.VMEM((128, CELLS), F32)
HOT = pltpu.VMEM((CELLS, SLOTS), BF16)
SPREAD = pltpu.VMEM((2 * STACK + 16, SLOTS), BF16)


def swapped(value, axes, first):
    count = lax.axis_size(axes)
    pairs = [(i, i + 1) for i in range(first, count - 1, 2)]
    return lax.ppermute(value, axes, pairs + [(above, below) for below, above in pairs])


def exchange(dom_odd, rim_chip, dom_even, rim_core):
    rim_chip = swapped(rim_chip, BLOCK, 1)
    dom_odd = swapped(dom_odd, DOM, 1)
    dom_even = swapped(dom_even, DOM, 0)
    rim_core = swapped(rim_core, BLOCK, 0)
    return dom_odd, rim_chip, dom_even, rim_core


def summed_over_blocks(sums):
    in_plane, along_z = lax.axis_size(PLANE), lax.axis_size("z")
    sums = lax.all_to_all(sums, PLANE, 0, 0, tiled=True)
    diagonal = [
        (z * in_plane + place, (z + place) % along_z * in_plane + place)
        for z in range(along_z)
        for place in range(along_z)
    ]
    other = lax.ppermute(jnp.sum(sums, axis=0, keepdims=True), BLOCK, diagonal)
    return lax.all_to_all(jnp.broadcast_to(other, sums.shape), PLANE, 0, 0, tiled=True)


def on_device(source, levels, ids, values, pairs, coarse, fine):
    levels, ids, values, coarse = (a.reshape(1, -1) for a in (levels, ids, values, coarse))
    table = jnp.asarray(packed_table())
    sends = [(FACE, CELLS), (128, SIDE), (FACE, CELLS), (128, SIDE)]
    params = (source, levels, ids, values, pairs, coarse, fine)
    *swapping, codes = call(
        first_kernel,
        [*sends, PACKED],
        [
            *(pltpu.VMEM(a.shape, a.dtype) for a in params),
            pltpu.VMEM((FIRST_ROWS, 256), BF16),
            FIELD,
            HOT,
            pltpu.SemaphoreType.DMA((8,)),
        ],
        *params,
        table,
        name="first",
        space=pl.ANY,
        limit=63,
    )

    arrays = [(128, CELLS), (TRACE, CELLS), (TRACE, CELLS), (FACE, PAIR_SLOTS)]
    scratch = [HOT, SPREAD, FIELD]
    arrived = exchange(*swapping)
    own = call(middle_kernel, arrays, [FIELD, PAIR_CODES], source, pairs, table, name="middle")
    image, *swapping, counts = call(
        image_kernel,
        [(128, CELLS), *sends, (16, CELLS)],
        scratch,
        codes,
        table,
        source,
        *own,
        *arrived,
        name="image",
    )
    arrived = exchange(*swapping)
    *own, first = call(
        middle_kernel, [*arrays, (FACE, PAIR_SLOTS)], [FIELD, PAIR_CODES], image, pairs, table, name="middle"
    )
    sums = call(
        moments_kernel,
        [(lax.axis_size(PLANE), 1, 128)],
        [],
        codes,
        table,
        image,
        *own,
        *arrived,
        *swapping,
        first,
        counts,
        source,
        name="moments",
    )[0]
    second = call(second_kernel, [(128, CELLS)], scratch, codes, table, image, *own, *arrived, name="second")[0]
    sums = summed_over_blocks(sums)
    return tuple(call(last_kernel, [source.shape] * 2, [], sums, source, image, second, name="last"))


def solution(mesh):
    dom, sub = mesh.devices.shape
    axes = BLOCK
    fine_mesh = Mesh(mesh.devices.reshape(dom // 4, 4, sub // 2, 2), axes)
    return jax.shard_map(
        on_device,
        mesh=fine_mesh,
        in_specs=(
            P(None, axes),
            P(axes),
            P(axes),
            P(),
            P(None, axes),
            P(axes),
            P(None, axes),
        ),
        out_specs=(P(None, axes), P(None, axes)),
        check_vma=False,
    )
```

```python
import jax
import jax.numpy as jnp
import numpy as np
import ml_dtypes
from jax import lax
from jax.experimental import pallas as pl
from jax.experimental.pallas import tpu as pltpu
from jax.sharding import Mesh, PartitionSpec as P

CELLS = 512
RIM = 64
EXTENT = CELLS + 2 * RIM
PAIRS = 960
PAIR_SLOTS = 1024
SIDE = 128
FACE = 32
MAIN = 24
TAIL = 6 * MAIN
STACK = TAIL + 8
TRACE = 160
FINE0 = PAIR_SLOTS
COARSE0 = PAIR_SLOTS + 4 * CELLS
SLOTS = COARSE0 + CELLS
CHUNK = 512
FINE_ROW = 2
COARSE_ROW = 6
SCALE_ROW = 8
PACKED = (16, PAIR_SLOTS)
TAU_PENALTY = 2.0
SIGMA_MASS = 4.0
BLOCK = ("z", "x", "y", "core")
DOM = ("z", "x")
PLANE = ("x", "y", "core")
F32 = jnp.float32
BF16 = jnp.bfloat16
ALONG_ROWS = (((1,), (0,)), ((), ()))
ALONG_LANES = (((1,), (1,)), ((), ()))


def element_tables():
    points = np.array([-1.0, -np.sqrt(3.0 / 7.0), 0.0, np.sqrt(3.0 / 7.0), 1.0])
    weights = np.array([0.1, 49.0 / 90.0, 32.0 / 45.0, 49.0 / 90.0, 0.1])

    def lagrange(location):
        values = np.ones((location.shape[0], 5))
        for column in range(5):
            for other in range(5):
                if other != column:
                    values[:, column] *= (location - points[other]) / (
                        points[column] - points[other]
                    )
        return values

    derivative = np.zeros((5, 5))
    for column in range(5):
        for other in range(5):
            if other != column:
                product = np.ones(5) / (points[column] - points[other])
                for remaining in range(5):
                    if remaining != column and remaining != other:
                        product = (
                            product
                            * (points - points[remaining])
                            / (points[column] - points[remaining])
                        )
                derivative[:, column] += product
    stiffness = derivative.T @ (weights[:, None] * derivative)
    halves = [lagrange((points - 1.0) / 2.0), lagrange((points + 1.0) / 2.0)]
    interp = [np.kron(halves[a], halves[b]) for a in range(2) for b in range(2)]
    return stiffness, weights, interp


def two_parts(table):
    high = table.astype(np.float32).astype(ml_dtypes.bfloat16)
    low = (table - high.astype(np.float64)).astype(np.float32).astype(ml_dtypes.bfloat16)
    return high, low


PLACES = {
    "trace": [(0, 0)],
    "up": [(160, 0), (160, 128)],
    "untrace": [(192, 0)],
    "coarse": [(320, 0), (480, 0)],
    "local": [(640, 0), (640, 128)],
    "down": [(768, 0), (768, 128)],
    "lumped": [(896, 0), (896, 128)],
}
FIRST_ROWS = 192
TABLE_ROWS = 1024


def packed_table():
    stiffness, weights, interp = element_tables()
    diag = np.diag(weights)

    def kron3(a, b, c):
        return np.kron(np.kron(a, b), c)

    local = np.zeros((128, 128))
    local[:125, :125] = (
        kron3(stiffness, diag, diag) + kron3(diag, stiffness, diag) + kron3(diag, diag, stiffness)
    )
    lumped = np.zeros((128, 1))
    lumped[:125, 0] = SIGMA_MASS * np.einsum("i,j,k->ijk", weights, weights, weights).reshape(-1)
    node = np.arange(125).reshape(5, 5, 5)
    slabs = [node[0], node[:, 0], node[:, :, 0], node[4], node[:, 4], node[:, :, 4]]
    stacked = np.concatenate([np.arange(6)[:, None] * MAIN + np.arange(MAIN), TAIL + np.arange(6)[:, None]], axis=1)
    trace = np.zeros((TRACE, 128))
    for face, slab in enumerate(slabs):
        trace[stacked[face], slab.reshape(-1)] = 1.0
    coarse = np.zeros((25, 25))
    down = np.zeros((4 * FACE, FACE))
    for child, matrix in enumerate(interp):
        coarse += matrix.T @ matrix
        down[child * FACE : child * FACE + 25, :25] = matrix
    coarse_stack = np.zeros((TRACE, TRACE))
    for rows in stacked:
        coarse_stack[np.ix_(rows, rows)] = TAU_PENALTY * coarse
    table = np.zeros((TABLE_ROWS, 256))
    places = {
        "trace": trace,
        "untrace": trace.T,
        "local": local,
        "coarse": coarse_stack,
        "down": -TAU_PENALTY * down,
        "up": -TAU_PENALTY * down.T,
        "lumped": lumped,
    }
    for name, value in places.items():
        parts = [value] if name.endswith("trace") else two_parts(value)
        for (row, lane), part in zip(PLACES[name], parts):
            table[row : row + value.shape[0], lane : lane + value.shape[1]] = part
    return table.astype(ml_dtypes.bfloat16)


def views(table):
    def view(name, rows, lanes):
        return [table.at[row : row + rows, lane : lane + lanes] for row, lane in PLACES[name]]

    return {
        "trace": view("trace", TRACE, 128)[0],
        "untrace": view("untrace", 128, TRACE)[0],
        "local": view("local", 128, 128),
        "coarse": view("coarse", TRACE, TRACE),
        "down": view("down", 4 * FACE, FACE),
        "up": view("up", FACE, 128),
        "lumped": view("lumped", 128, 1),
    }


def dot(a, b, dims=ALONG_ROWS):
    return lax.dot_general(a, b, dims, preferred_element_type=F32)


def split(value):
    high = value.astype(BF16)
    return high, (value - high.astype(F32)).astype(BF16)


def table_dot(parts, value):
    high, low = split(value)
    table = parts[0][...]
    return dot(table, high) + dot(table, low) + dot(parts[1][...], high)


def face_traces(trace_ref, field):
    high, low = split(field)
    table = trace_ref[...]
    return dot(table, high), dot(table, low)


def one_hot(cell, rows):
    place = lax.broadcasted_iota(jnp.int32, (rows, cell.shape[1]), 0)
    return jnp.where(place == cell, 1.0, 0.0).astype(BF16)


def pick(gathered, face):
    both = gathered[0:STACK] + gathered[STACK : 2 * STACK]
    main = None
    for f in range(6):
        term = jnp.where(face == f, both[f * MAIN : (f + 1) * MAIN], 0.0)
        main = term if main is None else main + term
    row = lax.broadcasted_iota(jnp.int32, (8, both.shape[1]), 0)
    last = jnp.sum(jnp.where(row == face, both[TAIL:STACK], 0.0), axis=0, keepdims=True)
    return jnp.concatenate([main, jnp.where(row == 0, last, 0.0)], axis=0)


def stack(value, face):
    row = lax.broadcasted_iota(jnp.int32, (8, value.shape[1]), 0)
    pieces = [jnp.where(face == f, value[0:MAIN], 0.0) for f in range(6)]
    return pieces + [jnp.where(row == face, value[MAIN : MAIN + 1], 0.0)]


def own_code(code):
    code = code.astype(jnp.int32)
    return code >> 9, code & (CELLS - 1)


def extended_code(code):
    code = code.astype(jnp.int32)
    face = jnp.where(code < 0, -1, 0)
    for f in range(1, 6):
        face = face + jnp.where(code >= f * EXTENT, 1, 0)
    return face, code - face * EXTENT - RIM


def padded_field(field_ref, field):
    if field_ref.shape[0] == 128:
        return field_ref[...]
    field[...] = jnp.zeros_like(field)
    field[0:125, :] = field_ref[...]
    return field[...]


def fine_code(codes, child):
    return own_code(codes[FINE_ROW + child : FINE_ROW + child + 1, 0:CELLS])


def coarse_code(codes):
    return own_code(codes[COARSE_ROW : COARSE_ROW + 1, 0:CELLS])


def gather_hanging(traces, hot, codes, up):
    rows = []
    for child in range(4):
        face, _ = fine_code(codes, child)
        start = FINE0 + child * CELLS
        rows.append(pick(dot(traces, hot[:, start : start + CELLS]), face))
    face, _ = coarse_code(codes)
    send_coarse = pick(dot(traces, hot[:, COARSE0:SLOTS]), face)
    send_fine = table_dot(up, jnp.concatenate(rows, axis=0))
    return send_coarse, send_fine


def hot_pairs(hot, codes):
    for start in range(0, PAIR_SLOTS, CHUNK):
        _, cell = own_code(codes[0:1, start : start + CHUNK])
        hot[:, start : start + CHUNK] = one_hot(cell, CELLS)


def hot_hanging(hot, codes):
    for child in range(4):
        _, cell = fine_code(codes, child)
        start = FINE0 + child * CELLS
        hot[:, start : start + CELLS] = one_hot(cell, CELLS)
    _, cell = coarse_code(codes)
    hot[:, COARSE0:SLOTS] = one_hot(cell, CELLS)


def joined(high, low):
    return jnp.concatenate([high[0:STACK], low[0:STACK]], axis=0).astype(BF16)


def stacked_traces(trace_ref, field):
    return joined(*face_traces(trace_ref, field))


def swaps(low, high, send_coarse, send_fine, dom_odd_ref, rim_ref, dom_even_ref):
    even_dom = lax.axis_index("x") % 2 == 0
    lane = lax.broadcasted_iota(jnp.int32, low.shape, 1)
    rim_ref[...] = jnp.where(lane < RIM, low, high)
    dom_even_ref[...] = jnp.where(even_dom, send_coarse, send_fine)
    dom_odd_ref[...] = jnp.where(even_dom, send_fine, send_coarse)


def first_kernel(*refs):
    field_in, level_in, id_in, values_in, pairs_in, coarse_in, fine_in, table_in = refs[:8]
    outs, codes = refs[8:11], refs[11]
    source, levels, ids, values, pairs, coarse, fine, table, field, hot, sems = refs[12:]
    moves = [
        (coarse_in, coarse),
        (fine_in, fine),
        (field_in, source),
        (table_in.at[0:FIRST_ROWS], table),
        (level_in, levels),
        (id_in, ids),
        (values_in, values),
        (pairs_in, pairs),
    ]
    copies = [pltpu.make_async_copy(*move, sems.at[i]) for i, move in enumerate(moves)]
    for copy in copies:
        copy.start()
    codes[...] = jnp.full(codes.shape, -1.0, F32)
    copies[0].wait()
    codes[COARSE_ROW : COARSE_ROW + 1, 0:CELLS] = coarse[...].astype(F32)
    copies[1].wait()
    codes[FINE_ROW : FINE_ROW + 4, 0:CELLS] = fine[...].astype(F32)
    hot_hanging(hot, codes)
    copies[2].wait()
    copies[3].wait()
    vector = padded_field(source, field)
    traces = stacked_traces(table.at[0:TRACE, 0:128], vector)
    up = [table.at[row : row + FACE, lane : lane + 128] for row, lane in PLACES["up"]]
    send_coarse, send_fine = gather_hanging(traces, hot, codes, up)
    swaps(vector[:, 0:SIDE], vector[:, CELLS - SIDE :], send_coarse, send_fine, *outs)
    for copy in copies[4:]:
        copy.wait()
    codes[0:2, 0:PAIRS] = pairs[...].astype(F32)
    place = lax.broadcasted_iota(jnp.int32, (values.shape[1], CELLS), 0)
    lookup = jnp.where(place == ids[...], 1.0, 0.0)
    coefficient = lax.dot_general(
        jnp.broadcast_to(values[...], (8, values.shape[1])),
        lookup,
        ALONG_ROWS,
        precision=lax.Precision.HIGHEST,
        preferred_element_type=F32,
    )
    level = levels[...]
    scale = jnp.where(level == 0, 1.0, jnp.where(level == 1, 0.5, 0.25))
    codes[SCALE_ROW : SCALE_ROW + 1, 0:CELLS] = coefficient[0:1] * scale
    codes[SCALE_ROW + 1 : SCALE_ROW + 2, 0:CELLS] = scale * scale * scale


def middle_kernel(
    field_ref, pairs_ref, table_ref, stiff_ref, trace_out_ref, coarse_out_ref, partner_ref, *refs
):
    *first_ref, field, pairs = refs
    pairs[...] = jnp.full(pairs.shape, -1, jnp.int32)
    pairs[0:2, 0:PAIRS] = pairs_ref[...]
    table = views(table_ref)
    vector = padded_field(field_ref, field)
    high, low = face_traces(table["trace"], vector)
    both = high + low
    trace_out_ref[...] = both
    coarse_out_ref[...] = table_dot(table["coarse"], both)
    traces = joined(high, low)
    for start in range(0, PAIR_SLOTS, CHUNK):
        face, cell = extended_code(pairs[1:2, start : start + CHUNK])
        partner_ref[:, start : start + CHUNK] = pick(dot(traces, one_hot(cell, CELLS)), face)
        for ref in first_ref:
            face, cell = own_code(pairs[0:1, start : start + CHUNK])
            ref[:, start : start + CHUNK] = pick(dot(traces, one_hot(cell, CELLS)), face)
    stiff_ref[...] = table_dot(table["local"], vector)


def applied(codes, table, stiff, field):
    rows = field.shape[0]
    lumped = [part[...][0:rows].astype(F32) for part in table["lumped"]]
    factor = codes[SCALE_ROW : SCALE_ROW + 1, 0:CELLS]
    cubed = codes[SCALE_ROW + 1 : SCALE_ROW + 2, 0:CELLS]
    return factor * stiff[0:rows] + cubed * ((lumped[0] + lumped[1]) * field)


def traces_beside(trace_ref, rim_chip_ref, rim_core_ref):
    is_below = lax.broadcasted_iota(jnp.int32, rim_chip_ref.shape, 1) >= SIDE - RIM
    from_chip = is_below == (lax.axis_index("core") == 0)
    return stacked_traces(trace_ref, jnp.where(from_chip, rim_chip_ref[...], rim_core_ref[...]))


def partner_values(codes, partner_ref, side_traces, start):
    face, cell = extended_code(codes[1:2, start : start + CHUNK])
    place = jnp.where(cell < 0, cell + SIDE, jnp.where(cell >= CELLS, cell - CELLS, -1))
    place = jnp.where(face < 0, -1, place)
    beside = pick(dot(side_traces, one_hot(place, SIDE)), face)
    return partner_ref[:, start : start + CHUNK] + beside


def add_faces(
    codes,
    table_ref,
    field_ref,
    stiff_ref,
    trace_in_ref,
    coarse_in_ref,
    partner_ref,
    dom_odd_ref,
    rim_chip_ref,
    dom_even_ref,
    rim_core_ref,
    hot,
    spread,
    local,
):
    table = views(table_ref)
    hot_pairs(hot, codes)
    hot_hanging(hot, codes)
    even_dom = lax.axis_index("x") % 2 == 0
    arriving = jnp.where(even_dom, dom_odd_ref[...], dom_even_ref[...])
    returned = jnp.where(even_dom, dom_even_ref[...], dom_odd_ref[...])
    side_traces = traces_beside(table["trace"], rim_chip_ref, rim_core_ref)

    def put(start, value, face, coarse):
        width = value.shape[1]
        high = value.astype(BF16).astype(F32)
        row = lax.broadcasted_iota(jnp.int32, (16, width), 0)
        count = jnp.where(row == (face + 8 if coarse else face), 1.0, 0.0)
        pieces = stack(high, face) + stack(value - high, face) + [count]
        spread[:, start : start + width] = jnp.concatenate(pieces, axis=0).astype(BF16)

    for start in range(0, PAIR_SLOTS, CHUNK):
        partner = partner_values(codes, partner_ref, side_traces, start)
        face, _ = own_code(codes[0:1, start : start + CHUNK])
        put(start, -TAU_PENALTY * partner, face, False)
    predicted = table_dot(table["down"], arriving)
    for child in range(4):
        face, _ = fine_code(codes, child)
        put(FINE0 + child * CELLS, predicted[child * FACE : (child + 1) * FACE], face, False)
    face, _ = coarse_code(codes)
    put(COARSE0, returned, face, True)
    added = dot(spread[...], hot[...], ALONG_LANES)
    both = added[0:STACK] + added[STACK : 2 * STACK]
    counts = added[2 * STACK : 2 * STACK + 16]
    pieces = [both[rows] + own for rows, own in own_faces(counts, trace_in_ref, coarse_in_ref)]
    pieces.append(jnp.zeros((TRACE - STACK, CELLS), F32))
    high, low = split(jnp.concatenate(pieces, axis=0))
    untrace = table["untrace"][...]
    rows = field_ref.shape[0]
    local[...] = dot(untrace, high) + dot(untrace, low)
    local[0:rows, :] += applied(codes, table, stiff_ref[...], field_ref[...])
    return local[...], counts


def own_faces(counts, trace_ref, coarse_ref):
    for f in range(7):
        rows = slice(f * MAIN, min((f + 1) * MAIN, STACK))
        fine = counts[f : f + 1] if f < 6 else counts[0:8]
        coarse = counts[f + 8 : f + 9] if f < 6 else counts[8:16]
        yield rows, (TAU_PENALTY * fine) * trace_ref[rows, :] + coarse * coarse_ref[rows, :]


def image_kernel(*refs):
    codes, table = refs[0], views(refs[1])
    image, counts = add_faces(*refs[:11], *refs[16:])
    refs[11][...] = image
    traces = stacked_traces(table["trace"], image)
    send_coarse, send_fine = gather_hanging(traces, refs[16], codes, table["up"])
    swaps(image[:, 0:SIDE], image[:, CELLS - SIDE :], send_coarse, send_fine, *refs[12:15])
    refs[15][...] = counts


def second_kernel(*refs):
    refs[11][...], _ = add_faces(*refs[:11], *refs[12:])


def total(value):
    return jnp.sum(jnp.sum(value, axis=0, keepdims=True), axis=1, keepdims=True)


def moments_kernel(
    codes,
    table_ref,
    image_ref,
    stiff_ref,
    trace_ref,
    coarse_ref,
    partner_ref,
    dom_odd_ref,
    rim_chip_ref,
    dom_even_ref,
    rim_core_ref,
    sent_odd_ref,
    _sent_rim_ref,
    sent_even_ref,
    first_ref,
    counts_ref,
    source_ref,
    sums_ref,
):
    table = views(table_ref)
    source = source_ref[...]
    image = image_ref[...]
    side_traces = traces_beside(table["trace"], rim_chip_ref, rim_core_ref)
    curved = total(image * applied(codes, table, stiff_ref[...], image))
    hanging = sent_odd_ref[...] * dom_odd_ref[...] + sent_even_ref[...] * dom_even_ref[...]
    for start in range(0, PAIR_SLOTS, CHUNK):
        partner = partner_values(codes, partner_ref, side_traces, start)
        hanging = hanging - TAU_PENALTY * (partner * first_ref[:, start : start + CHUNK])
    curved = curved + total(hanging)
    own = [trace_ref[rows, :] * value for rows, value in own_faces(counts_ref[...], trace_ref, coarse_ref)]
    curved = curved + total(jnp.concatenate(own, axis=0))
    sums = [total(source * source), total(source * image[0:125]), total(image * image), curved]
    lane = lax.broadcasted_iota(jnp.int32, (1, 128), 1)
    line = jnp.zeros((1, 128), F32)
    for index, value in enumerate(sums):
        line = line + jnp.where(lane == index, value, 0.0)
    sums_ref[...] = jnp.broadcast_to(line[None], sums_ref.shape)


def last_kernel(sums_ref, source_ref, image_ref, second_ref, solution_ref, residual_ref):
    line = jnp.sum(sums_ref[...], axis=0)
    rr, rw, ww, wu = (line[:, i : i + 1] for i in range(4))
    first_step = rr / rw
    rr_next = rr - 2.0 * first_step * rw + first_step * first_step * ww
    grown = 1.0 + rr_next / rr
    curvature = (
        grown * grown * rw - 2.0 * first_step * grown * ww + first_step * first_step * wu
    )
    second_step = rr_next / curvature
    p = first_step + second_step * grown
    q = second_step * first_step
    source = source_ref[...]
    image = image_ref[0:125, :]
    solution_ref[...] = p * source - q * image
    residual_ref[...] = source - p * image + q * second_ref[0:125, :]


def call(kernel, out_shapes, scratch, *operands, name, space=pltpu.VMEM, limit=48):
    return pl.pallas_call(
        kernel,
        out_shape=[jax.ShapeDtypeStruct(shape, F32) for shape in out_shapes],
        in_specs=[pl.BlockSpec(memory_space=space)] * len(operands),
        out_specs=[pl.BlockSpec(memory_space=pltpu.VMEM)] * len(out_shapes),
        scratch_shapes=scratch,
        compiler_params=pltpu.CompilerParams(vmem_limit_bytes=limit * 1024 * 1024),
        name=name,
    )(*operands)


PAIR_CODES = pltpu.VMEM((8, PAIR_SLOTS), jnp.int32)
FIELD = pltpu.VMEM((128, CELLS), F32)
HOT = pltpu.VMEM((CELLS, SLOTS), BF16)
SPREAD = pltpu.VMEM((2 * STACK + 16, SLOTS), BF16)


def swapped(value, axes, first):
    count = lax.axis_size(axes)
    pairs = [(i, i + 1) for i in range(first, count - 1, 2)]
    return lax.ppermute(value, axes, pairs + [(above, below) for below, above in pairs])


def exchange(dom_odd, rim, dom_even):
    rim_chip = swapped(rim, BLOCK, 1)
    dom_odd = swapped(dom_odd, DOM, 1)
    dom_even = swapped(dom_even, DOM, 0)
    rim_core = swapped(rim, BLOCK, 0)
    return dom_odd, rim_chip, dom_even, rim_core


def summed_over_blocks(sums):
    in_plane, along_z = lax.axis_size(PLANE), lax.axis_size("z")
    sums = lax.all_to_all(sums, PLANE, 0, 0, tiled=True)
    diagonal = [
        (z * in_plane + place, (z + place) % along_z * in_plane + place)
        for z in range(along_z)
        for place in range(along_z)
    ]
    other = lax.ppermute(jnp.sum(sums, axis=0, keepdims=True), BLOCK, diagonal)
    return lax.all_to_all(jnp.broadcast_to(other, sums.shape), PLANE, 0, 0, tiled=True)


def on_device(source, levels, ids, values, pairs, coarse, fine):
    levels, ids, values, coarse = (a.reshape(1, -1) for a in (levels, ids, values, coarse))
    table = jnp.asarray(packed_table())
    sends = [(FACE, CELLS), (128, SIDE), (FACE, CELLS)]
    params = (source, levels, ids, values, pairs, coarse, fine)
    *swapping, codes = call(
        first_kernel,
        [*sends, PACKED],
        [
            *(pltpu.VMEM(a.shape, a.dtype) for a in params),
            pltpu.VMEM((FIRST_ROWS, 256), BF16),
            FIELD,
            HOT,
            pltpu.SemaphoreType.DMA((8,)),
        ],
        *params,
        table,
        name="first",
        space=pl.ANY,
        limit=63,
    )

    arrays = [(128, CELLS), (TRACE, CELLS), (TRACE, CELLS), (FACE, PAIR_SLOTS)]
    scratch = [HOT, SPREAD, FIELD]
    arrived = exchange(*swapping)
    own = call(middle_kernel, arrays, [FIELD, PAIR_CODES], source, pairs, table, name="middle")
    image, *swapping, counts = call(
        image_kernel,
        [(128, CELLS), *sends, (16, CELLS)],
        scratch,
        codes,
        table,
        source,
        *own,
        *arrived,
        name="image",
    )
    arrived = exchange(*swapping)
    *own, first = call(
        middle_kernel, [*arrays, (FACE, PAIR_SLOTS)], [FIELD, PAIR_CODES], image, pairs, table, name="middle"
    )
    sums = call(
        moments_kernel,
        [(lax.axis_size(PLANE), 1, 128)],
        [],
        codes,
        table,
        image,
        *own,
        *arrived,
        *swapping,
        first,
        counts,
        source,
        name="moments",
    )[0]
    second = call(second_kernel, [(128, CELLS)], scratch, codes, table, image, *own, *arrived, name="second")[0]
    sums = summed_over_blocks(sums)
    return tuple(call(last_kernel, [source.shape] * 2, [], sums, source, image, second, name="last"))


def solution(mesh):
    dom, sub = mesh.devices.shape
    axes = BLOCK
    fine_mesh = Mesh(mesh.devices.reshape(dom // 4, 4, sub // 2, 2), axes)
    return jax.shard_map(
        on_device,
        mesh=fine_mesh,
        in_specs=(
            P(None, axes),
            P(axes),
            P(axes),
            P(),
            P(None, axes),
            P(axes),
            P(None, axes),
        ),
        out_specs=(P(None, axes), P(None, axes)),
        check_vma=False,
    )
```
